512 devices in a mesh: brick: 128 (over z, x, core), slab: 4 (over y).
Axes of the slice: x: 4, y: 4, z: 16, core: 2. Of those that a mesh axis runs over, the one named last changes fastest.
Arguments:
- adjoint_end: float32 [3, 4194304], P(None, ('brick', 'slab')), may hold values from -6 to 6
- positions: float32 [2, 3, 4194304], P(None, None, ('brick', 'slab')), may hold values from 0.5 to 2.5
- tile_brick: int32 [2, 32768], P(None, ('brick', 'slab')), may hold values from 0 to 127
- tile_fill: int32 [32768], P(('brick', 'slab')), may hold values from 4 to 128, as said below
- send_rows: int32 [512, 256], P(('brick', 'slab')), may hold values from 0 to 8192, as said below
- source_rows: int32 [4194304], P(('brick', 'slab')), may hold values from 0 to 8447, as said below
- ckpt_mass: float32 [65536, 128], P(('brick', 'slab')), may hold values from 0.5 to 4
- ckpt_velocity: float32 [65536, 384], P(('brick', 'slab')), may hold values from -6 to 6
- ckpt_target: int32 [65536], P(('brick', 'slab')), may hold values from 0 to 255, as said below
- ckpt_brick: int32 [65536], P(('brick', 'slab')), may hold values from 0 to 127, as said below
- gripper_axis: float32 [3], replicated, may hold values from 0.5 to 1
Outputs:
- adjoint_start: float32 [3, 4194304], P(None, ('brick', 'slab'))
The draws below stay inside these ranges and needn't reach their ends.
Inputs may be any that keep to these rules, and one draw needn't show every extreme that they name: `tile_fill`: counted from a tile's first row; the first tile of every device is full. `send_rows`: distinct live rows of the device's second layout; the first 128 go to the previous device along brick, the rest to the next; 8192 marks every slot exactly where that neighbour does not exist, and no other. `source_rows`: A row of the first layout takes its own row of the second layout unless that row was sent; each sent row's place takes exactly one received slot, and every received slot from an existing neighbour is used once. Both layouts share tile_fill. `ckpt_target`: values of one device are distinct; the backward owner has the sender's slab index; a device sends 0, 1 or 2 bricks to each peer, in slots from 0. `ckpt_brick`: each backward owner receives each of its 128 bricks exactly once.
All inputs are finite; a program needn't handle non-finite values.
Results may differ from the reference program's by a relative error of at most 0.00065.
Values sent between devices are 32-bit elements; how exact they have to be, the bound alone decides.
A program may use at most 64 MiB of HBM per device.

```python
import math
import jax
import jax.numpy as jnp
from jax import lax

TILE = 128
BZ = 4
BY = 4
BX = 8
TILES_DEV = 64
SUBSTEPS = 2
NB = 128
ROWS_DEV = 8192
CAPR = 128
CAPB = 2
BRICKS = 65536
ROWS_ALL = 4194304
N_BRICK = 128
N_SLAB = 4
DEVICES = 512


def layout_plan(key):
    fill_key = jax.random.fold_in(key, 101)
    score_key = jax.random.fold_in(key, 102)
    fills = jax.random.randint(fill_key, (DEVICES, TILES_DEV), 4, TILE + 1).astype(jnp.int32)
    fills = fills.at[:, 0].set(TILE)
    live_rows = (jnp.arange(TILE)[None, None, :] < fills[:, :, None]).reshape(DEVICES, ROWS_DEV)
    draws = jax.random.randint(score_key, (DEVICES, ROWS_DEV), 0, 1024).astype(jnp.int32)
    scores = jnp.where(live_rows, draws, 1024) * ROWS_DEV + jnp.arange(ROWS_DEV, dtype=jnp.int32)[None, :]
    ranking = jnp.argsort(scores, axis=1, stable=True).astype(jnp.int32)
    to_left = ranking[:, :CAPR]
    to_right = ranking[:, CAPR:2 * CAPR]
    brick_index = jnp.arange(DEVICES, dtype=jnp.int32) // N_SLAB
    has_left = (brick_index > 0)[:, None]
    has_right = (brick_index < N_BRICK - 1)[:, None]
    sending = jnp.concatenate([jnp.where(has_left, to_left, ROWS_DEV), jnp.where(has_right, to_right, ROWS_DEV)], axis=1).astype(jnp.int32)
    slot_ids = jnp.arange(CAPR, dtype=jnp.int32)[None, :]
    device_ids = jnp.arange(DEVICES, dtype=jnp.int32)[:, None]
    source = jnp.broadcast_to(jnp.arange(ROWS_DEV, dtype=jnp.int32)[None, :], (DEVICES, ROWS_DEV))
    source = source.at[device_ids, to_left].set(jnp.where(has_left, ROWS_DEV + slot_ids, to_left))
    source = source.at[device_ids, to_right].set(jnp.where(has_right, ROWS_DEV + CAPR + slot_ids, to_right))
    return (fills.reshape(-1), sending, source.reshape(-1).astype(jnp.int32))


def owner_core(key):
    group_size = NB // N_BRICK
    offset_key = jax.random.fold_in(key, 201)
    group_key = jax.random.fold_in(key, 202)
    shuffle_key = jax.random.fold_in(key, 203)
    quarter = N_BRICK // 4
    half_axis = N_BRICK // 2
    base_perm = jax.random.permutation(offset_key, N_BRICK).astype(jnp.int32)
    offsets_perm = ((base_perm - base_perm[0] + half_axis) % N_BRICK).astype(jnp.int32)
    offsets = jnp.concatenate([offsets_perm[:quarter], offsets_perm[:quarter], offsets_perm[quarter:quarter + N_BRICK // 2]])
    offsets = offsets[jax.random.permutation(group_key, N_BRICK)].astype(jnp.int32)
    group_ids = jnp.arange(N_BRICK, dtype=jnp.int32)
    same_offset = offsets[:, None] == offsets[None, :]
    repeat_rank = jnp.sum(jnp.where(same_offset & (group_ids[None, :] < group_ids[:, None]), 1, 0), axis=1).astype(jnp.int32)
    draws = jax.random.randint(shuffle_key, (DEVICES, NB), 0, 1024).astype(jnp.int32)
    shuffle = jnp.argsort(draws * NB + jnp.arange(NB, dtype=jnp.int32)[None, :], axis=1, stable=True).astype(jnp.int32)
    forward = jnp.arange(DEVICES, dtype=jnp.int32)
    forward_brick = forward // N_SLAB
    forward_slab = forward % N_SLAB
    local_rows = jnp.arange(NB, dtype=jnp.int32)
    group_of = local_rows // group_size
    within = local_rows % group_size
    peer_index = (forward_brick[:, None] - offsets[group_of][None, :]) % N_BRICK
    target = peer_index * CAPB + repeat_rank[group_of][None, :] * group_size + within[None, :]
    backward = peer_index * N_SLAB + forward_slab[:, None]
    brick_ids = shuffle[backward, jnp.broadcast_to(local_rows[None, :], (DEVICES, NB))]
    half_group = jnp.min(jnp.where(offsets == half_axis, group_ids, N_BRICK)).astype(jnp.int32)
    linked_row = (half_group * group_size).astype(jnp.int32)
    linked = shuffle[:, linked_row].astype(jnp.int32)
    return (target.reshape(-1).astype(jnp.int32), brick_ids.reshape(-1).astype(jnp.int32), linked)


def owner_plan(key):
    target, brick_ids, linked = owner_core(key)
    return (target, brick_ids)


def tile_plan(key):
    linked = owner_core(key)[2]
    planted = jnp.array([0, BX - 1, (BZ - 1) * BY * BX + BX - 1, NB - 1], dtype=jnp.int32)
    layers = []
    for substep in range(SUBSTEPS):
        rest_key = jax.random.fold_in(key, 301 + substep)
        rest = jax.random.randint(rest_key, (DEVICES, TILES_DEV - 5), 0, NB).astype(jnp.int32)
        fixed_part = jnp.broadcast_to(planted[None, :], (DEVICES, 4))
        layer = jnp.concatenate([linked[:, None], fixed_part, rest], axis=1)
        layers.append(layer.reshape(-1))
    return jnp.stack(layers, axis=0).astype(jnp.int32)


def draw_tile_brick(key, part):
    return tile_plan(key)


def draw_tile_fill(key, part):
    return layout_plan(key)[0]


def draw_send_rows(key, part):
    return layout_plan(key)[1]


def draw_source_rows(key, part):
    return layout_plan(key)[2]


def draw_ckpt_target(key, part):
    return owner_plan(key)[0]


def draw_ckpt_brick(key, part):
    return owner_plan(key)[1]


def shard_levels(key, shape, pieces, smallest, high):
    def one(dim, blocks):
        heights = jax.random.uniform(jax.random.fold_in(jax.random.fold_in(key, 6), dim), (blocks,), jnp.float32, smallest / len(pieces), high / len(pieces))
        return jnp.repeat(jnp.exp(heights), shape[dim] // blocks).reshape((-1,) + (1,) * (len(shape) - dim - 1))

    level = one(*pieces[0])
    for cut in pieces[1:]:
        level = level * one(*cut)
    return level


def scatter_about(own_key, dims, width, most, pieces=(), kind=jnp.bfloat16):
    values = width * jax.random.normal(own_key, dims, jnp.float32)
    if pieces:
        values = values * shard_levels(own_key, dims, pieces, -0.22, 0.18)
    return jnp.clip(values, -most, most).astype(kind)


def setup_inputs(seed: int = 0) -> dict:
    splits = jax.random.split(jax.random.key(seed), 12)
    adjoint_end = scatter_about(splits[0], (3, ROWS_ALL), 1.0, 6.0, ((1, 512),), jnp.float32)
    positions = jnp.clip(0.5 + 2.0 * jax.random.uniform(splits[1], (SUBSTEPS, 3, ROWS_ALL), jnp.float32) ** shard_levels(splits[1], (SUBSTEPS, 3, ROWS_ALL), ((2, 512),), -0.2, 0.2), 0.5, 2.5)
    tile_brick = draw_tile_brick(jax.random.fold_in(splits[11], 71), 0)
    tile_fill = draw_tile_fill(jax.random.fold_in(splits[11], 71), 0)
    send_rows = draw_send_rows(jax.random.fold_in(splits[11], 71), 0)
    source_rows = draw_source_rows(jax.random.fold_in(splits[11], 71), 0)
    ckpt_mass = jnp.clip(jnp.exp(math.log(4.0) - 2.0794415 * jax.random.uniform(splits[6], (BRICKS, 128), jnp.float32) ** shard_levels(splits[6], (BRICKS, 128), ((0, 512),), -0.2, 0.2)), 0.5, 4.0)
    ckpt_velocity = scatter_about(splits[7], (BRICKS, 384), 1.0, 6.0, ((0, 512),), jnp.float32)
    ckpt_target = draw_ckpt_target(jax.random.fold_in(splits[11], 71), 0)
    ckpt_brick = draw_ckpt_brick(jax.random.fold_in(splits[11], 71), 0)
    gripper_axis = jnp.clip(jax.random.uniform(splits[10], (3,), jnp.float32, 0.5, 1.0), 0.5, 1.0)
    return {"adjoint_end": adjoint_end, "positions": positions, "tile_brick": tile_brick, "tile_fill": tile_fill, "send_rows": send_rows, "source_rows": source_rows, "ckpt_mass": ckpt_mass, "ckpt_velocity": ckpt_velocity, "ckpt_target": ckpt_target, "ckpt_brick": ckpt_brick, "gripper_axis": gripper_axis}


diffusion = 0.15

def bspline(offset):
    magnitude = jnp.abs(offset)
    inner = 0.75 - offset * offset
    outer = 0.5 * (1.5 - magnitude) * (1.5 - magnitude)
    return jnp.where(magnitude < 0.5, inner, jnp.where(magnitude < 1.5, outer, jnp.zeros_like(offset)))

def row_weights(position, fills):
    tile_count = fills.shape[0]
    node_axis = jnp.arange(4).astype(position.dtype)
    along_z = bspline(position[0][None, :] - node_axis[:, None])
    along_y = bspline(position[1][None, :] - node_axis[:, None])
    along_x = bspline(position[2][None, :] - node_axis[:, None])
    weights = along_z[:, None, None, :] * along_y[None, :, None, :] * along_x[None, None, :, :]
    weights = weights.reshape(64, tile_count * TILE)
    live_rows = (jnp.arange(TILE)[None, :] < fills[:, None]).reshape(tile_count * TILE)
    return jnp.where(live_rows[None, :], weights, jnp.zeros_like(weights))

def brick_table(bricks):
    return (jnp.arange(NB)[:, None] == bricks[None, :]).astype(jnp.float32)

def to_grid(weights, adjoint, bricks):
    tile_count = bricks.shape[0]
    per_tile = jnp.einsum('ntr,ctr->cnt', weights.reshape(64, tile_count, TILE), adjoint.reshape(3, tile_count, TILE), precision=lax.Precision.HIGHEST)
    return jnp.einsum('cnt,lt->cnl', per_tile, brick_table(bricks).astype(per_tile.dtype), precision=lax.Precision.HIGHEST)

def to_rows(weights, grid_adj, bricks):
    tile_count = bricks.shape[0]
    per_tile = jnp.einsum('cnl,lt->cnt', grid_adj, brick_table(bricks).astype(grid_adj.dtype), precision=lax.Precision.HIGHEST)
    rows_out = jnp.einsum('ntr,cnt->ctr', weights.reshape(64, tile_count, TILE), per_tile, precision=lax.Precision.HIGHEST)
    return rows_out.reshape(3, tile_count * TILE)

def stencil(padded):
    center = padded[:, 1:-1, 1:-1, 1:-1]
    beside = padded[:, 1:-1, 1:-1, 2:] + padded[:, 1:-1, 1:-1, :-2]
    beside = beside + padded[:, 1:-1, 2:, 1:-1] + padded[:, 1:-1, :-2, 1:-1]
    beside = beside + padded[:, 2:, 1:-1, 1:-1] + padded[:, :-2, 1:-1, 1:-1]
    return center + diffusion * (beside - 6.0 * center)

def assemble(grid_adj):
    local = grid_adj.reshape(DEVICES, 3, 4, 4, 4, BZ, BY, BX).transpose(0, 1, 5, 2, 6, 3, 7, 4)
    local = local.reshape(N_BRICK, N_SLAB, 3, 4 * BZ, 4 * BY, 4 * BX)
    return local.transpose(2, 3, 1, 4, 0, 5).reshape(3, 4 * BZ, N_SLAB * 4 * BY, N_BRICK * 4 * BX)

def disassemble(node_field):
    local = node_field.reshape(3, 4 * BZ, N_SLAB, 4 * BY, N_BRICK, 4 * BX).transpose(4, 2, 0, 1, 3, 5)
    local = local.reshape(DEVICES, 3, BZ, 4, BY, 4, BX, 4).transpose(0, 1, 3, 5, 7, 2, 4, 6)
    return local.reshape(DEVICES, 3, 64, NB)

def migrate(adjoint, send_rows, source_rows):
    padded = jnp.concatenate([adjoint, jnp.zeros((DEVICES, 3, 1), adjoint.dtype)], axis=2)
    outgoing = jax.vmap(lambda packed, chosen: packed[:, chosen])(padded, send_rows)
    outgoing = outgoing.reshape(N_BRICK, N_SLAB, 3, 2 * CAPR)
    empty_block = jnp.zeros((1, N_SLAB, 3, CAPR), adjoint.dtype)
    from_left = jnp.concatenate([empty_block, outgoing[:-1, :, :, CAPR:]], axis=0)
    from_right = jnp.concatenate([outgoing[1:, :, :, :CAPR], empty_block], axis=0)
    candidates = jnp.concatenate([adjoint.reshape(N_BRICK, N_SLAB, 3, ROWS_DEV), from_left, from_right], axis=3)
    candidates = candidates.reshape(DEVICES, 3, ROWS_DEV + 2 * CAPR)
    source = source_rows.reshape(DEVICES, ROWS_DEV)
    return jax.vmap(lambda packed, chosen: packed[:, chosen])(candidates, source)

def reference(adjoint_end, positions, tile_brick, tile_fill, send_rows, source_rows, ckpt_mass, ckpt_velocity, ckpt_target, ckpt_brick, gripper_axis):
    normal = gripper_axis / jnp.sqrt(jnp.sum(gripper_axis * gripper_axis))
    row_ids = jnp.arange(BRICKS).astype(jnp.int32)
    forward = row_ids // NB
    slab_of = forward % N_SLAB
    destination = ((ckpt_target // CAPB * N_SLAB + slab_of) * NB + ckpt_brick).astype(jnp.int32)
    mass_all = jnp.zeros((BRICKS, 128), ckpt_mass.dtype).at[destination].set(ckpt_mass).reshape(DEVICES, NB, 2, 64)
    velocity = jnp.zeros((BRICKS, 384), ckpt_velocity.dtype).at[destination].set(ckpt_velocity).reshape(DEVICES, NB, 2, 3, 64)
    normal_speed = normal[0] * velocity[:, :, :, 0] + normal[1] * velocity[:, :, :, 1] + normal[2] * velocity[:, :, :, 2]
    fills = tile_fill.reshape(DEVICES, TILES_DEV)
    adjoint = adjoint_end.reshape(3, DEVICES, ROWS_DEV).transpose(1, 0, 2)
    for substep in (1, 0):
        position = positions[substep].reshape(3, DEVICES, ROWS_DEV).transpose(1, 0, 2)
        bricks = tile_brick[substep].reshape(DEVICES, TILES_DEV)
        grid_adj = lax.map(lambda packed: to_grid(row_weights(packed[0], packed[1]), packed[2], packed[3]), (position, fills, adjoint, bricks))
        node_field = assemble(grid_adj)
        padded = jnp.pad(node_field, ((0, 0), (1, 1), (1, 1), (1, 1)))
        smoothed = disassemble(stencil(padded))
        grid_mass = mass_all[:, :, substep].transpose(0, 2, 1)
        speed_now = normal_speed[:, :, substep].transpose(0, 2, 1)
        project = normal[0] * smoothed[:, 0] + normal[1] * smoothed[:, 1] + normal[2] * smoothed[:, 2]
        contact = jnp.where(speed_now < 0.0, jnp.ones_like(speed_now), jnp.zeros_like(speed_now))
        corrected = smoothed - contact[:, None] * normal[None, :, None, None] * project[:, None]
        scaled = corrected / grid_mass[:, None]
        adjoint = lax.map(lambda packed: to_rows(row_weights(packed[0], packed[1]), packed[2], packed[3]), (position, fills, scaled, bricks))
        if substep == 1:
            adjoint = migrate(adjoint, send_rows, source_rows)
    return adjoint.transpose(1, 0, 2).reshape(3, ROWS_ALL)
```

```python
import jax
import jax.numpy as jnp
from jax import lax
from jax.experimental import pallas as pl
from jax.experimental.pallas import tpu as pltpu
from jax.sharding import PartitionSpec as P

TILE = 128
TILES = 64
GROUPS = 8
NZ = 16
NXC = 8
N_BRICK = 128
N_SLAB = 4
BLOCK = 40

diffusion = 0.15
F32 = jnp.float32
BF16 = jnp.bfloat16
MESH = pl.DeviceIdType.MESH


def contract_last(left, right):
    return lax.dot_general(left, right, (((1,), (1,)), ((), ())), preferred_element_type=F32)


def contract_first(left, right):
    return lax.dot_general(left, right, (((0,), (0,)), ((), ())), preferred_element_type=F32)


def split(value):
    high = value.astype(BF16)
    low = (value - high.astype(F32)).astype(BF16)
    return high, low


def iota(shape, dim):
    return lax.broadcasted_iota(jnp.int32, shape, dim)


def bspline(offset):
    magnitude = jnp.abs(offset)
    inner = 0.75 - offset * offset
    tail = 1.5 - magnitude
    outer = 0.5 * tail * tail
    return jnp.where(magnitude < 0.5, inner, jnp.where(magnitude < 1.5, outer, 0.0))


def kernel(
    adj_ref, pos_ref, tile_ref, fill_ref, send_ref, source_ref, mass_ref, vel_ref,
    target_ref, brick_ref, axis_ref, out_ref,
    weights, rows, per_tile, grid, xsum, ext,
    s1a, r1a, s1b, r1b, s2a, r2a, s2b, r2b,
    xs, xr, ys, yr, ms, mr,
    a1s, a1r, b1s, b1r, a2s, a2r, b2s, b2r, hs, hr, gs, gr,
):
    b = lax.axis_index("brick")
    s = lax.axis_index("slab")
    z = lax.div(b, NXC)
    xc = lax.rem(b, NXC)
    left = lax.rem(b + N_BRICK - 1, N_BRICK)
    right = lax.rem(b + 1, N_BRICK)
    down = lax.rem(s + N_SLAB - 1, N_SLAB)
    up = lax.rem(s + 1, N_SLAB)

    def near(d):
        return lax.rem(xc + d, NXC)

    def far(d):
        return lax.rem(z + d, NZ)

    barrier = pltpu.get_barrier_semaphore()

    def greet_near(d, carry):
        pl.semaphore_signal(barrier, inc=1, device_id=(z * NXC + near(d), s), device_id_type=MESH)
        return carry

    def greet_far(d, carry):
        pl.semaphore_signal(barrier, inc=1, device_id=(far(d) * NXC + xc, s), device_id_type=MESH)
        return carry

    lax.fori_loop(1, NXC, greet_near, 0)
    lax.fori_loop(1, NZ, greet_far, 0)
    for who in ((left, s), (right, s), (b, down), (b, up)):
        pl.semaphore_signal(barrier, inc=1, device_id=who, device_id_type=MESH)

    def remote(src, dst, send, recv, who):
        return pltpu.make_async_remote_copy(
            src_ref=src, dst_ref=dst, send_sem=send, recv_sem=recv, device_id=who,
            device_id_type=MESH,
        )

    def near_copy(src, dst, send, recv, d):
        to = near(d)
        return remote(
            src.at[pl.ds(pl.multiple_of(to * BLOCK, 8), BLOCK)],
            dst.at[pl.ds(pl.multiple_of(xc * BLOCK, 8), BLOCK)],
            send.at[d], recv.at[d], (z * NXC + to, s),
        )

    def far_copy(src, dst, send, recv, d):
        to = far(d)
        return remote(src.at[to], dst.at[z], send.at[d], recv.at[d], (to * NXC + xc, s))

    def run(count, act):
        def body(d, carry):
            act(d)
            return carry

        lax.fori_loop(1, count, body, 0)

    lane = iota((8, 128), 1)
    axis = [jnp.full((1, 128), axis_ref[c], F32) for c in range(3)]
    length = jnp.sqrt(axis[0] * axis[0] + axis[1] * axis[1] + axis[2] * axis[2])
    normal = [a / length for a in axis]
    lane_q = iota((128, 128), 1)
    v0 = vel_ref[:, 0:128]
    v1 = vel_ref[:, 128:256]
    v2 = vel_ref[:, 256:384]
    speed_first = normal[0] * v0 + normal[1] * pltpu.roll(v0, 64, 1) + normal[2] * v1
    speed_second = normal[0] * v1 + normal[1] * pltpu.roll(v2, 64, 1) + normal[2] * v2
    speed = jnp.where(lane_q < 64, speed_first, speed_second)
    contact = jnp.where(speed < 0.0, 1.0, 0.0)
    mass_turned = pltpu.roll(mass_ref[...], 64, 1)
    packed_a = jnp.where(lane_q < 64, mass_turned, contact)
    packed_b = jnp.where(lane_q < 64, contact, mass_turned)
    both = jnp.concatenate([packed_a, packed_b], axis=1)
    high, low = split(both)
    target = target_ref[...]
    slot = lax.bitwise_and(target, 1)
    peer = lax.shift_right_logical(target, 1)
    peer_near = lax.bitwise_and(peer, NXC - 1)
    within = slot * NZ + lax.shift_right_logical(peer, 3)
    place = peer_near * 32 + within
    chosen = jnp.where(iota((256, 128), 0) == place, 1.0, 0.0).astype(BF16)
    packed = jnp.dot(
        jnp.concatenate([chosen, chosen], axis=1), jnp.concatenate([high, low], axis=0),
        preferred_element_type=F32,
    )
    index_left = jnp.where(
        iota((16, 128), 0) == peer_near, (brick_ref[...] + 1).astype(F32), 0.0
    ).astype(BF16)
    index_right = jnp.where(iota((128, 128), 0) == within, 1.0, 0.0).astype(BF16)
    index_out = contract_last(index_left, index_right)
    for i in range(NXC):
        s1a[BLOCK * i:BLOCK * i + 32, :] = packed[32 * i:32 * i + 32, 0:128]
        s1a[BLOCK * i + 32:BLOCK * i + 40, :] = jnp.broadcast_to(index_out[i:i + 1], (8, 128))
        s1b[BLOCK * i:BLOCK * i + 32, :] = packed[32 * i:32 * i + 32, 128:256]
        s1b[BLOCK * i + 32:BLOCK * i + 40, :] = jnp.zeros((8, 128), F32)

    pl.semaphore_wait(barrier, NXC - 1 + NZ - 1 + 4)
    run(NXC, lambda d: near_copy(s1a, r1a, a1s, a1r, d).start())
    run(NXC, lambda d: near_copy(s1b, r1b, b1s, b1r, d).start())
    own = pl.ds(pl.multiple_of(xc * BLOCK, 8), BLOCK)
    r1a[own] = s1a[own]
    r1b[own] = s1b[own]

    def spread(t, carry):
        block = adj_ref[:, pl.ds(pl.multiple_of(t * TILE, TILE), TILE)]
        for c in range(3):
            rows[c, pl.ds(t, 1), :] = block[c:c + 1]
        return carry

    lax.fori_loop(0, TILES, spread, 0, unroll=8)

    sub = iota((8, 128), 0)
    node_x = lax.bitwise_and(sub, 3).astype(F32)
    node_y = lax.shift_right_logical(sub, 2).astype(F32)
    row48 = lax.bitwise_and(iota((48, 128), 0), 7)

    def build(k, g):
        for i in range(8):
            t = g * 8 + i
            at = pl.ds(pl.multiple_of(t * TILE, TILE), TILE)
            pz, py, px = (
                jnp.broadcast_to(pos_ref[k, c:c + 1, at], (8, 128)) for c in range(3)
            )
            pz = jnp.where(lane < fill_ref[0, t], pz, 100.0)
            wx = bspline(px - node_x)
            wz = bspline(pz - node_x)
            xy = [bspline(py - node_y) * wx, bspline(py - (node_y + 2.0)) * wx]
            value = jnp.concatenate(
                [jnp.broadcast_to(wz[n:n + 1], (8, 128)) * xy[h] for n in range(4) for h in range(2)],
                axis=0,
            )
            high, low = split(value)
            weights[k, t, :, 0:128] = high
            weights[k, t, :, 128:256] = low

    def to_grid(k, g):
        at = pl.ds(pl.multiple_of(g * 8, 8), 8)
        parts = [rows[c, at, :] for c in range(3)]
        value = jnp.concatenate(parts, axis=0)
        high = value.astype(BF16).astype(F32)
        value = jnp.concatenate([high, value - high], axis=0)
        lhs = jnp.concatenate(
            [jnp.where(row48 == i, value, 0.0).astype(BF16) for i in range(8)], axis=1
        )
        rhs = jnp.concatenate(
            [
                jnp.concatenate(
                    [weights[k, g * 8 + i, :, 0:128], weights[k, g * 8 + i, :, 128:256]], axis=0
                )
                for i in range(8)
            ],
            axis=1,
        )
        found = contract_last(lhs, rhs)
        found = found[0:24] + found[24:48]
        for c in range(3):
            per_tile[c, at, :] = found[8 * c:8 * c + 8]

    def table(k):
        line = jnp.broadcast_to(tile_ref[k:k + 1, :].astype(F32), (TILES, TILES))
        mine = iota((TILES, TILES), 0) == iota((TILES, TILES), 1)
        column = jnp.sum(jnp.where(mine, line, 0.0), axis=1, keepdims=True)
        return jnp.where(iota((TILES, 128), 1).astype(F32) == column, 1.0, 0.0).astype(BF16)

    def sum_bricks(tiles):
        value = jnp.concatenate([per_tile[c] for c in range(3)], axis=1)
        high, low = split(value)
        found = contract_first(
            jnp.concatenate([high, low], axis=0), jnp.concatenate([tiles, tiles], axis=0)
        )
        for c in range(3):
            grid[64 * c:64 * c + 64, :] = (
                found[128 * c:128 * c + 64] + found[128 * c + 64:128 * c + 128]
            )

    def halo(k):
        x_high = remote(xs.at[k, 0], xr.at[k, 0], hs.at[k, 0], hr.at[k, 0], (right, s))
        x_low = remote(xs.at[k, 1], xr.at[k, 1], hs.at[k, 1], hr.at[k, 1], (left, s))
        y_high = remote(ys.at[k, 0], yr.at[k, 0], hs.at[k, 2], hr.at[k, 2], (b, up))
        y_low = remote(ys.at[k, 1], yr.at[k, 1], hs.at[k, 3], hr.at[k, 3], (b, down))
        return x_high, x_low, y_high, y_low

    def send_halo(k):
        xs[k, 0] = grid[pl.ds(3, 48, stride=4), :]
        xs[k, 1] = grid[pl.ds(0, 48, stride=4), :]
        cells = grid[...].reshape(12, 16, 128)
        ys[k, 0] = cells[:, 12:16]
        ys[k, 1] = cells[:, 0:4]
        for copy in halo(k):
            copy.start()

    brick_lane = iota((1, 128), 1)
    lane_x = lax.bitwise_and(brick_lane, 7)
    lane_y = lax.bitwise_and(lax.shift_right_logical(brick_lane, 3), 3)
    lane_z = lax.shift_right_logical(brick_lane, 5)
    has_left = jnp.where(b > 0, 1.0, 0.0)
    has_right = jnp.where(b < N_BRICK - 1, 1.0, 0.0)
    has_down = jnp.where(s > 0, 1.0, 0.0)
    has_up = jnp.where(s < N_SLAB - 1, 1.0, 0.0)

    def smooth(k):
        planes = [grid[pl.ds(j, 48, stride=4), :] for j in range(4)]
        before = jnp.where(
            lane_x == 0, pltpu.roll(xr[k, 0] * has_left, 121, 1), pltpu.roll(planes[3], 1, 1)
        )
        after = jnp.where(
            lane_x == 7, pltpu.roll(xr[k, 1] * has_right, 7, 1), pltpu.roll(planes[0], 127, 1)
        )
        line = [before] + planes + [after]
        for j in range(4):
            xsum[pl.ds(j, 48, stride=4), :] = line[j] + line[j + 2]
        cells = grid[...].reshape(12, 16, 128)
        low = pltpu.roll((yr[k, 0] * has_down), 104, 2)
        high = pltpu.roll((yr[k, 1] * has_up), 24, 2)
        lane_y3 = lane_y.reshape(1, 1, 128)
        below = jnp.where(lane_y3 == 0, low, pltpu.roll(cells[:, 12:16], 8, 2))
        above = jnp.where(lane_y3 == 3, high, pltpu.roll(cells[:, 0:4], 120, 2))
        ysum = jnp.concatenate([cells[:, 4:16], above], axis=1) + jnp.concatenate(
            [below, cells[:, 0:12]], axis=1
        )
        out = []
        for c in range(3):
            base = grid[64 * c:64 * c + 64, :]
            last = jnp.where(lane_z == 0, 0.0, pltpu.roll(base[48:64], 32, 1))
            first = jnp.where(lane_z == 3, 0.0, pltpu.roll(base[0:16], 96, 1))
            zsum = jnp.concatenate([base[16:64], first], axis=0) + jnp.concatenate(
                [last, base[0:48]], axis=0
            )
            beside = (
                xsum[64 * c:64 * c + 64, :] + ysum[4 * c:4 * c + 4].reshape(64, 128) + zsum
            )
            out.append(base + diffusion * (beside - 6.0 * base))
        return out

    def relay(src, dst):
        for i in range(NZ):
            dst[i, 0:8, :] = src[pl.ds(i, 8, stride=BLOCK), :]
            dst[i, 8:16, :] = src[pl.ds(16 + i, 8, stride=BLOCK), :]

    def by_node(got, place):
        value = got.reshape(256, 128)
        high, low = split(value)
        return contract_first(
            jnp.concatenate([high, low], axis=0), jnp.concatenate([place, place], axis=0)
        )

    def correct(cells, mass, touch, tiles):
        project = normal[0] * cells[0] + normal[1] * cells[1] + normal[2] * cells[2]
        scaled = [(cells[c] - touch * normal[c] * project) / mass for c in range(3)]
        highs, lows = zip(*(split(value) for value in scaled))
        stack = jnp.concatenate(
            [part for half in (highs, lows) for value in half for part in (value, value)], axis=0
        )
        found = contract_last(tiles, stack)
        for i in range(6):
            ext[i] = found[:, 128 * i:128 * i + 128]

    pair_of = lax.bitwise_and(iota((8, 128), 0), 7) * 64
    lane_pair = lax.bitwise_and(lane, 64)

    def to_rows(k, g):
        at = pl.ds(pl.multiple_of(g * 8, 8), 8)
        parts = [ext[i, at, :] for i in range(6)]
        lhs = jnp.concatenate(
            [
                jnp.concatenate(
                    [jnp.where(pair_of == lane_pair + 128 * j, part, 0.0) for part in parts], axis=0
                ).astype(BF16)
                for j in range(4)
            ],
            axis=1,
        )
        rhs = jnp.concatenate([weights[k, g * 8 + i] for i in range(8)], axis=0)
        found = jnp.dot(lhs, rhs, preferred_element_type=F32)
        return found[0:24, 0:128] + found[24:48, 0:128] + found[0:24, 128:256]

    def first_pass(g, carry):
        build(1, g)
        to_grid(1, g)
        return carry

    lax.fori_loop(0, GROUPS, first_pass, 0)
    tiles_b = table(1)
    sum_bricks(tiles_b)
    send_halo(1)

    run(NXC, lambda d: near_copy(s1a, r1a, a1s, a1r, d).wait_recv())
    relay(r1a, s2a)
    index_in = r1a[pl.ds(32, 8, stride=BLOCK), :]
    index_two = jnp.concatenate([index_in, pltpu.roll(index_in, 112, 1)], axis=0)
    index_two = jnp.where(iota((16, 128), 1) < NZ, index_two, 0.0).astype(BF16)
    pick = jnp.where(iota((NZ, 128), 0) == iota((NZ, 128), 1), 1.0, 0.0).astype(BF16)
    index_far = contract_last(
        pick, jnp.concatenate([index_two, jnp.zeros((112, 128), BF16)], axis=0)
    )
    for i in range(NZ):
        s2a[i, 16:17, :] = index_far[i:i + 1]
    run(NZ, lambda d: far_copy(s2a, r2a, a2s, a2r, d).start())
    r2a[z] = s2a[z]

    def second_weights(g, carry):
        build(0, g)
        return carry

    lax.fori_loop(0, GROUPS, second_weights, 0)
    tiles_a = table(0)

    for copy in halo(1):
        copy.wait_recv()
    cells = smooth(1)

    run(NXC, lambda d: near_copy(s1b, r1b, b1s, b1r, d).wait_recv())
    relay(r1b, s2b)
    r2b[z] = s2b[z]

    run(NZ, lambda d: far_copy(s2a, r2a, a2s, a2r, d).wait_recv())
    run(NZ, lambda d: far_copy(s2b, r2b, b2s, b2r, d).start())
    index_row = jnp.concatenate([r2a[i, 16:17, :] for i in range(NZ)], axis=0)
    spread_index = jnp.concatenate(
        [jnp.broadcast_to(index_row[i:i + 1], (16, 128)) for i in range(NZ)], axis=0
    )
    mine = lax.bitwise_and(iota((256, 128), 0), 15) == iota((256, 128), 1)
    column = jnp.sum(jnp.where(mine, spread_index, 0.0), axis=1, keepdims=True) - 1.0
    placed = jnp.where(iota((256, 128), 1).astype(F32) == column, 1.0, 0.0).astype(BF16)
    nodes_b = by_node(jnp.concatenate([r2a[i, 0:16, :] for i in range(NZ)], axis=0), placed)
    correct(cells, nodes_b[0:64], nodes_b[64:128], tiles_b)

    def second_rows(g, carry):
        found = to_rows(1, g)
        for c in range(3):
            rows[c, pl.ds(pl.multiple_of(g * 8, 8), 8), :] = found[8 * c:8 * c + 8]
        return carry

    lax.fori_loop(0, GROUPS, second_rows, 0)

    for side in range(2):
        wanted = send_ref[:, 128 * side:128 * side + 128]
        which = jnp.broadcast_to(lax.bitwise_and(wanted, 127), (8, 128))
        tile = lax.shift_right_logical(wanted, 7)
        for c in range(3):
            total = jnp.zeros((8, 128), F32)
            for v in range(8):
                found = jnp.take_along_axis(
                    rows[c, 8 * v:8 * v + 8, :], which, axis=1, mode="promise_in_bounds"
                )
                total = total + jnp.where(sub + 8 * v == tile, found, 0.0)
            ms[side, c:c + 1, :] = jnp.sum(total, axis=0, keepdims=True)
    go_left = remote(ms.at[0], mr.at[1], gs.at[0], gr.at[0], (left, s))
    go_right = remote(ms.at[1], mr.at[0], gs.at[1], gr.at[1], (right, s))
    go_left.start()
    go_right.start()
    go_left.wait_recv()
    go_right.wait_recv()
    for v in range(8):
        source = source_ref[8 * v:8 * v + 8, :]
        which = lax.bitwise_and(source, 127)
        for c in range(3):
            at_left, at_right = (
                jnp.take_along_axis(
                    jnp.broadcast_to(mr[side, c:c + 1, :], (8, 128)), which, axis=1,
                    mode="promise_in_bounds",
                )
                for side in range(2)
            )
            kept = rows[c, 8 * v:8 * v + 8, :]
            rows[c, 8 * v:8 * v + 8, :] = jnp.where(
                source < 8192, kept, jnp.where(source < 8320, at_left, at_right)
            )

    def third_pass(g, carry):
        to_grid(0, g)
        return carry

    lax.fori_loop(0, GROUPS, third_pass, 0)
    sum_bricks(tiles_a)
    send_halo(0)
    run(NZ, lambda d: far_copy(s2b, r2b, b2s, b2r, d).wait_recv())
    nodes_a = by_node(r2b[...], placed)
    for copy in halo(0):
        copy.wait_recv()
    correct(smooth(0), nodes_a[64:128], nodes_a[0:64], tiles_a)

    def last_rows(g, carry):
        found = to_rows(0, g)
        for i in range(8):
            at = pl.ds(pl.multiple_of((g * 8 + i) * TILE, TILE), TILE)
            for c in range(3):
                out_ref[c:c + 1, at] = found[8 * c + i:8 * c + i + 1]
        return carry

    lax.fori_loop(0, GROUPS, last_rows, 0)

    run(NXC, lambda d: near_copy(s1a, r1a, a1s, a1r, d).wait_send())
    run(NXC, lambda d: near_copy(s1b, r1b, b1s, b1r, d).wait_send())
    run(NZ, lambda d: far_copy(s2a, r2a, a2s, a2r, d).wait_send())
    run(NZ, lambda d: far_copy(s2b, r2b, b2s, b2r, d).wait_send())
    for copy in halo(1) + halo(0) + (go_left, go_right):
        copy.wait_send()


def per_device(
    adjoint_end, positions, tile_brick, tile_fill, send_rows, source_rows,
    ckpt_mass, ckpt_velocity, ckpt_target, ckpt_brick, gripper_axis,
):
    vmem = pl.BlockSpec(memory_space=pltpu.VMEM)
    smem = pl.BlockSpec(memory_space=pltpu.SMEM)
    dma = pltpu.SemaphoreType.DMA
    return pl.pallas_call(
        kernel,
        out_shape=jax.ShapeDtypeStruct((3, TILES * TILE), F32),
        in_specs=[vmem, vmem, vmem, smem, vmem, vmem, vmem, vmem, vmem, vmem, smem],
        out_specs=vmem,
        scratch_shapes=[
            pltpu.VMEM((2, TILES, 64, 256), BF16),
            pltpu.VMEM((3, TILES, TILE), F32),
            pltpu.VMEM((3, TILES, 128), F32),
            pltpu.VMEM((192, 128), F32),
            pltpu.VMEM((192, 128), F32),
            pltpu.VMEM((6, TILES, 128), F32),
            pltpu.VMEM((NXC * BLOCK, 128), F32),
            pltpu.VMEM((NXC * BLOCK, 128), F32),
            pltpu.VMEM((NXC * BLOCK, 128), F32),
            pltpu.VMEM((NXC * BLOCK, 128), F32),
            pltpu.VMEM((NZ, 17, 128), F32),
            pltpu.VMEM((NZ, 17, 128), F32),
            pltpu.VMEM((NZ, 16, 128), F32),
            pltpu.VMEM((NZ, 16, 128), F32),
            pltpu.VMEM((2, 2, 48, 128), F32),
            pltpu.VMEM((2, 2, 48, 128), F32),
            pltpu.VMEM((2, 2, 12, 4, 128), F32),
            pltpu.VMEM((2, 2, 12, 4, 128), F32),
            pltpu.VMEM((2, 3, 128), F32),
            pltpu.VMEM((2, 3, 128), F32),
            dma((NXC,)), dma((NXC,)), dma((NXC,)), dma((NXC,)),
            dma((NZ,)), dma((NZ,)), dma((NZ,)), dma((NZ,)),
            dma((2, 4)), dma((2, 4)), dma((2,)), dma((2,)),
        ],
        compiler_params=pltpu.CompilerParams(
            collective_id=0, has_side_effects=True, vmem_limit_bytes=48 * 1024 * 1024
        ),
        cost_estimate=pl.CostEstimate(
            flops=200_000_000, bytes_accessed=1_000_000, transcendentals=0
        ),
        name="substeps",
    )(
        adjoint_end, positions, tile_brick, tile_fill.reshape(1, TILES), send_rows,
        source_rows.reshape(TILES, TILE), ckpt_mass, ckpt_velocity,
        ckpt_target.reshape(1, 128), ckpt_brick.reshape(1, 128), gripper_axis,
    )


def solution(mesh):
    return jax.shard_map(
        per_device,
        mesh=mesh,
        in_specs=(
            P(None, ("brick", "slab")),
            P(None, None, ("brick", "slab")),
            P(None, ("brick", "slab")),
            P(("brick", "slab")),
            P(("brick", "slab"), None),
            P(("brick", "slab")),
            P(("brick", "slab"), None),
            P(("brick", "slab"), None),
            P(("brick", "slab")),
            P(("brick", "slab")),
            P(),
        ),
        out_specs=P(None, ("brick", "slab")),
        check_vma=False,
    )
```

```python
import jax
import jax.numpy as jnp
from jax import lax
from jax.experimental import pallas as pl
from jax.experimental.pallas import tpu as pltpu
from jax.sharding import PartitionSpec as P

TILE = 128
TILES = 64
GROUPS = 8
NZ = 16
NXC = 8
N_BRICK = 128
N_SLAB = 4
BLOCK = 40

diffusion = 0.15
F32 = jnp.float32
BF16 = jnp.bfloat16
MESH = pl.DeviceIdType.MESH


def contract_last(left, right):
    return lax.dot_general(left, right, (((1,), (1,)), ((), ())), preferred_element_type=F32)


def contract_first(left, right):
    return lax.dot_general(left, right, (((0,), (0,)), ((), ())), preferred_element_type=F32)


def split(value):
    high = value.astype(BF16)
    low = (value - high.astype(F32)).astype(BF16)
    return high, low


def iota(shape, dim):
    return lax.broadcasted_iota(jnp.int32, shape, dim)


def bspline(offset):
    magnitude = jnp.abs(offset)
    inner = 0.75 - offset * offset
    tail = 1.5 - magnitude
    outer = 0.5 * tail * tail
    return jnp.where(magnitude < 0.5, inner, jnp.where(magnitude < 1.5, outer, 0.0))


def kernel(
    adj_hbm, pos_hbm, tile_hbm, fill_hbm, send_hbm, source_hbm, mass_hbm, vel_hbm,
    target_hbm, brick_hbm, axis_hbm, out_ref,
    adj_ref, pos_ref, tile_ref, fill_ref, send_ref, source_ref, mass_ref, vel_ref,
    target_ref, brick_ref, axis_ref, load_sem,
    weights, rows, per_tile, grid, xsum, ext,
    s1a, r1a, s1b, r1b, s2a, r2a, s2b, r2b,
    xs, xr, ys, yr, ms, mr,
    a1s, a1r, b1s, b1r, a2s, a2r, b2s, b2r, hs, hr, gs, gr,
):
    b = lax.axis_index("brick")
    s = lax.axis_index("slab")
    z = lax.div(b, NXC)
    xc = lax.rem(b, NXC)
    left = lax.rem(b + N_BRICK - 1, N_BRICK)
    right = lax.rem(b + 1, N_BRICK)
    down = lax.rem(s + N_SLAB - 1, N_SLAB)
    up = lax.rem(s + 1, N_SLAB)

    def near(d):
        return lax.rem(xc + d, NXC)

    def far(d):
        turn = lax.div(d, 2) * (1 - 2 * lax.rem(d, 2))
        return lax.rem(z + NZ + NZ // 2 + turn, NZ)

    barrier = pltpu.get_barrier_semaphore()

    def greet_near(d, carry):
        pl.semaphore_signal(barrier, inc=1, device_id=(z * NXC + near(d), s), device_id_type=MESH)
        return carry

    def greet_far(d, carry):
        pl.semaphore_signal(barrier, inc=1, device_id=(far(d) * NXC + xc, s), device_id_type=MESH)
        return carry

    lax.fori_loop(1, NZ, greet_far, 0)
    lax.fori_loop(1, NXC, greet_near, 0)
    for who in ((left, s), (right, s), (b, down), (b, up)):
        pl.semaphore_signal(barrier, inc=1, device_id=who, device_id_type=MESH)

    loads = [
        pltpu.make_async_copy(src, dst, load_sem.at[i])
        for i, (src, dst) in enumerate((
            (axis_hbm, axis_ref), (vel_hbm, vel_ref), (mass_hbm, mass_ref),
            (target_hbm, target_ref), (brick_hbm, brick_ref), (adj_hbm, adj_ref),
            (pos_hbm, pos_ref), (fill_hbm, fill_ref), (tile_hbm, tile_ref),
            (send_hbm, send_ref), (source_hbm, source_ref),
        ))
    ]
    for load in loads:
        load.start()
    for load in loads[0:5]:
        load.wait()

    def remote(src, dst, send, recv, who):
        return pltpu.make_async_remote_copy(
            src_ref=src, dst_ref=dst, send_sem=send, recv_sem=recv, device_id=who,
            device_id_type=MESH,
        )

    def near_copy(src, dst, send, recv, d):
        to = near(d)
        return remote(
            src.at[pl.ds(pl.multiple_of(to * BLOCK, 8), BLOCK)],
            dst.at[pl.ds(pl.multiple_of(xc * BLOCK, 8), BLOCK)],
            send.at[d], recv.at[d], (z * NXC + to, s),
        )

    def far_copy(src, dst, send, recv, d):
        to = far(d)
        return remote(src.at[to], dst.at[z], send.at[d], recv.at[d], (to * NXC + xc, s))

    def run(count, act):
        def body(d, carry):
            act(d)
            return carry

        lax.fori_loop(1, count, body, 0)

    lane = iota((8, 128), 1)
    axis = [jnp.full((1, 128), axis_ref[0, c], F32) for c in range(3)]
    length = jnp.sqrt(axis[0] * axis[0] + axis[1] * axis[1] + axis[2] * axis[2])
    normal = [a / length for a in axis]
    lane_q = iota((128, 128), 1)
    v0 = vel_ref[:, 0:128]
    v1 = vel_ref[:, 128:256]
    v2 = vel_ref[:, 256:384]
    speed_first = normal[0] * v0 + normal[1] * pltpu.roll(v0, 64, 1) + normal[2] * v1
    speed_second = normal[0] * v1 + normal[1] * pltpu.roll(v2, 64, 1) + normal[2] * v2
    speed = jnp.where(lane_q < 64, speed_first, speed_second)
    contact = jnp.where(speed < 0.0, 1.0, 0.0)
    mass_turned = pltpu.roll(mass_ref[...], 64, 1)
    packed_a = jnp.where(lane_q < 64, mass_turned, contact)
    packed_b = jnp.where(lane_q < 64, contact, mass_turned)
    both = jnp.concatenate([packed_a, packed_b], axis=1)
    high, low = split(both)
    target = target_ref[...]
    slot = lax.bitwise_and(target, 1)
    peer = lax.shift_right_logical(target, 1)
    peer_near = lax.bitwise_and(peer, NXC - 1)
    within = slot * NZ + lax.shift_right_logical(peer, 3)
    place = peer_near * 32 + within
    chosen = jnp.where(iota((256, 128), 0) == place, 1.0, 0.0).astype(BF16)
    packed = jnp.dot(
        jnp.concatenate([chosen, chosen], axis=1), jnp.concatenate([high, low], axis=0),
        preferred_element_type=F32,
    )
    index_left = jnp.where(
        iota((16, 128), 0) == peer_near, (brick_ref[...] + 1).astype(F32), 0.0
    ).astype(BF16)
    index_right = jnp.where(iota((128, 128), 0) == within, 1.0, 0.0).astype(BF16)
    index_out = contract_last(index_left, index_right)
    for i in range(NXC):
        s1a[BLOCK * i:BLOCK * i + 32, :] = packed[32 * i:32 * i + 32, 0:128]
        s1a[BLOCK * i + 32:BLOCK * i + 40, :] = jnp.broadcast_to(index_out[i:i + 1], (8, 128))
        s1b[BLOCK * i:BLOCK * i + 32, :] = packed[32 * i:32 * i + 32, 128:256]
        s1b[BLOCK * i + 32:BLOCK * i + 40, :] = jnp.zeros((8, 128), F32)

    pl.semaphore_wait(barrier, NXC - 1 + NZ - 1 + 4)
    run(NXC, lambda d: near_copy(s1a, r1a, a1s, a1r, d).start())
    run(NXC, lambda d: near_copy(s1b, r1b, b1s, b1r, d).start())
    own = pl.ds(pl.multiple_of(xc * BLOCK, 8), BLOCK)
    r1a[own] = s1a[own]
    r1b[own] = s1b[own]

    for load in loads[5:11]:
        load.wait()

    def spread(t, carry):
        block = adj_ref[:, pl.ds(pl.multiple_of(t * TILE, TILE), TILE)]
        for c in range(3):
            rows[c, pl.ds(t, 1), :] = block[c:c + 1]
        return carry

    lax.fori_loop(0, TILES, spread, 0, unroll=8)

    sub = iota((8, 128), 0)
    node_x = lax.bitwise_and(sub, 3).astype(F32)
    node_y = lax.shift_right_logical(sub, 2).astype(F32)
    row48 = lax.bitwise_and(iota((48, 128), 0), 7)

    def build(k, g):
        for i in range(8):
            t = g * 8 + i
            at = pl.ds(pl.multiple_of(t * TILE, TILE), TILE)
            pz, py, px = (
                jnp.broadcast_to(pos_ref[c, k:k + 1, at], (8, 128)) for c in range(3)
            )
            pz = jnp.where(lane < fill_ref[0, t], pz, 100.0)
            wx = bspline(px - node_x)
            wz = bspline(pz - node_x)
            xy = [bspline(py - node_y) * wx, bspline(py - (node_y + 2.0)) * wx]
            value = jnp.concatenate(
                [jnp.broadcast_to(wz[n:n + 1], (8, 128)) * xy[h] for n in range(4) for h in range(2)],
                axis=0,
            )
            high, low = split(value)
            weights[k, t, :, 0:128] = high
            weights[k, t, :, 128:256] = low

    def to_grid(k, g):
        at = pl.ds(pl.multiple_of(g * 8, 8), 8)
        parts = [rows[c, at, :] for c in range(3)]
        value = jnp.concatenate(parts, axis=0)
        high = value.astype(BF16).astype(F32)
        value = jnp.concatenate([high, value - high], axis=0)
        lhs = jnp.concatenate(
            [jnp.where(row48 == i, value, 0.0).astype(BF16) for i in range(8)], axis=1
        )
        rhs = jnp.concatenate(
            [
                jnp.concatenate(
                    [weights[k, g * 8 + i, :, 0:128], weights[k, g * 8 + i, :, 128:256]], axis=0
                )
                for i in range(8)
            ],
            axis=1,
        )
        found = contract_last(lhs, rhs)
        found = found[0:24] + found[24:48]
        for c in range(3):
            per_tile[c, at, :] = found[8 * c:8 * c + 8]

    def table(k):
        line = jnp.broadcast_to(tile_ref[k:k + 1, :].astype(F32), (TILES, TILES))
        mine = iota((TILES, TILES), 0) == iota((TILES, TILES), 1)
        column = jnp.sum(jnp.where(mine, line, 0.0), axis=1, keepdims=True)
        return jnp.where(iota((TILES, 128), 1).astype(F32) == column, 1.0, 0.0).astype(BF16)

    def sum_bricks(tiles):
        value = jnp.concatenate([per_tile[c] for c in range(3)], axis=1)
        high, low = split(value)
        found = contract_first(
            jnp.concatenate([high, low], axis=0), jnp.concatenate([tiles, tiles], axis=0)
        )
        for c in range(3):
            grid[64 * c:64 * c + 64, :] = (
                found[128 * c:128 * c + 64] + found[128 * c + 64:128 * c + 128]
            )

    def halo(k):
        x_high = remote(xs.at[k, 0], xr.at[k, 0], hs.at[k, 0], hr.at[k, 0], (right, s))
        x_low = remote(xs.at[k, 1], xr.at[k, 1], hs.at[k, 1], hr.at[k, 1], (left, s))
        y_high = remote(ys.at[k, 0], yr.at[k, 0], hs.at[k, 2], hr.at[k, 2], (b, up))
        y_low = remote(ys.at[k, 1], yr.at[k, 1], hs.at[k, 3], hr.at[k, 3], (b, down))
        return x_high, x_low, y_high, y_low

    def send_halo(k):
        xs[k, 0] = grid[pl.ds(3, 48, stride=4), :]
        xs[k, 1] = grid[pl.ds(0, 48, stride=4), :]
        cells = grid[...].reshape(12, 16, 128)
        ys[k, 0] = cells[:, 12:16]
        ys[k, 1] = cells[:, 0:4]
        for copy in halo(k):
            copy.start()

    brick_lane = iota((1, 128), 1)
    lane_x = lax.bitwise_and(brick_lane, 7)
    lane_y = lax.bitwise_and(lax.shift_right_logical(brick_lane, 3), 3)
    lane_z = lax.shift_right_logical(brick_lane, 5)
    has_left = jnp.where(b > 0, 1.0, 0.0)
    has_right = jnp.where(b < N_BRICK - 1, 1.0, 0.0)
    has_down = jnp.where(s > 0, 1.0, 0.0)
    has_up = jnp.where(s < N_SLAB - 1, 1.0, 0.0)

    def smooth(k):
        planes = [grid[pl.ds(j, 48, stride=4), :] for j in range(4)]
        before = jnp.where(
            lane_x == 0, pltpu.roll(xr[k, 0] * has_left, 121, 1), pltpu.roll(planes[3], 1, 1)
        )
        after = jnp.where(
            lane_x == 7, pltpu.roll(xr[k, 1] * has_right, 7, 1), pltpu.roll(planes[0], 127, 1)
        )
        line = [before] + planes + [after]
        for j in range(4):
            xsum[pl.ds(j, 48, stride=4), :] = line[j] + line[j + 2]
        cells = grid[...].reshape(12, 16, 128)
        low = pltpu.roll((yr[k, 0] * has_down), 104, 2)
        high = pltpu.roll((yr[k, 1] * has_up), 24, 2)
        lane_y3 = lane_y.reshape(1, 1, 128)
        below = jnp.where(lane_y3 == 0, low, pltpu.roll(cells[:, 12:16], 8, 2))
        above = jnp.where(lane_y3 == 3, high, pltpu.roll(cells[:, 0:4], 120, 2))
        ysum = jnp.concatenate([cells[:, 4:16], above], axis=1) + jnp.concatenate(
            [below, cells[:, 0:12]], axis=1
        )
        out = []
        for c in range(3):
            base = grid[64 * c:64 * c + 64, :]
            last = jnp.where(lane_z == 0, 0.0, pltpu.roll(base[48:64], 32, 1))
            first = jnp.where(lane_z == 3, 0.0, pltpu.roll(base[0:16], 96, 1))
            zsum = jnp.concatenate([base[16:64], first], axis=0) + jnp.concatenate(
                [last, base[0:48]], axis=0
            )
            beside = (
                xsum[64 * c:64 * c + 64, :] + ysum[4 * c:4 * c + 4].reshape(64, 128) + zsum
            )
            out.append(base + diffusion * (beside - 6.0 * base))
        return out

    def relay(src, dst):
        for i in range(NZ):
            dst[i, 0:8, :] = src[pl.ds(i, 8, stride=BLOCK), :]
            dst[i, 8:16, :] = src[pl.ds(16 + i, 8, stride=BLOCK), :]

    def by_node(got, place):
        value = got.reshape(256, 128)
        high, low = split(value)
        return contract_first(
            jnp.concatenate([high, low], axis=0), jnp.concatenate([place, place], axis=0)
        )

    def correct(cells, mass, touch, tiles):
        project = normal[0] * cells[0] + normal[1] * cells[1] + normal[2] * cells[2]
        scaled = [(cells[c] - touch * normal[c] * project) / mass for c in range(3)]
        highs, lows = zip(*(split(value) for value in scaled))
        stack = jnp.concatenate(
            [part for half in (highs, lows) for value in half for part in (value, value)], axis=0
        )
        found = contract_last(tiles, stack)
        for i in range(6):
            ext[i] = found[:, 128 * i:128 * i + 128]

    pair_of = lax.bitwise_and(iota((8, 128), 0), 7) * 64
    lane_pair = lax.bitwise_and(lane, 64)

    def to_rows(k, g):
        at = pl.ds(pl.multiple_of(g * 8, 8), 8)
        parts = [ext[i, at, :] for i in range(6)]
        lhs = jnp.concatenate(
            [
                jnp.concatenate(
                    [jnp.where(pair_of == lane_pair + 128 * j, part, 0.0) for part in parts], axis=0
                ).astype(BF16)
                for j in range(4)
            ],
            axis=1,
        )
        rhs = jnp.concatenate([weights[k, g * 8 + i] for i in range(8)], axis=0)
        found = jnp.dot(lhs, rhs, preferred_element_type=F32)
        return found[0:24, 0:128] + found[24:48, 0:128] + found[0:24, 128:256]

    def first_pass(g, carry):
        build(1, g)
        to_grid(1, g)
        return carry

    lax.fori_loop(0, GROUPS, first_pass, 0, unroll=2)
    tiles_b = table(1)
    sum_bricks(tiles_b)
    send_halo(1)

    run(NXC, lambda d: near_copy(s1a, r1a, a1s, a1r, d).wait_recv())
    relay(r1a, s2a)
    index_in = r1a[pl.ds(32, 8, stride=BLOCK), :]
    index_two = jnp.concatenate([index_in, pltpu.roll(index_in, 112, 1)], axis=0)
    index_two = jnp.where(iota((16, 128), 1) < NZ, index_two, 0.0).astype(BF16)
    pick = jnp.where(iota((NZ, 128), 0) == iota((NZ, 128), 1), 1.0, 0.0).astype(BF16)
    index_far = contract_last(
        pick, jnp.concatenate([index_two, jnp.zeros((112, 128), BF16)], axis=0)
    )
    for i in range(NZ):
        s2a[i, 16:17, :] = index_far[i:i + 1]
    run(NZ, lambda d: far_copy(s2a, r2a, a2s, a2r, d).start())
    r2a[z] = s2a[z]

    run(NXC, lambda d: near_copy(s1b, r1b, b1s, b1r, d).wait_recv())
    relay(r1b, s2b)
    r2b[z] = s2b[z]
    run(NZ, lambda d: far_copy(s2b, r2b, b2s, b2r, d).start())

    def second_weights(g, carry):
        build(0, g)
        return carry

    lax.fori_loop(0, GROUPS, second_weights, 0, unroll=2)
    tiles_a = table(0)

    for copy in halo(1):
        copy.wait_recv()
    cells = smooth(1)


    run(NZ, lambda d: far_copy(s2a, r2a, a2s, a2r, d).wait_recv())
    index_row = jnp.concatenate([r2a[i, 16:17, :] for i in range(NZ)], axis=0)
    spread_index = jnp.concatenate(
        [jnp.broadcast_to(index_row[i:i + 1], (16, 128)) for i in range(NZ)], axis=0
    )
    mine = lax.bitwise_and(iota((256, 128), 0), 15) == iota((256, 128), 1)
    column = jnp.sum(jnp.where(mine, spread_index, 0.0), axis=1, keepdims=True) - 1.0
    placed = jnp.where(iota((256, 128), 1).astype(F32) == column, 1.0, 0.0).astype(BF16)
    nodes_b = by_node(jnp.concatenate([r2a[i, 0:16, :] for i in range(NZ)], axis=0), placed)
    correct(cells, nodes_b[0:64], nodes_b[64:128], tiles_b)

    def second_rows(g, carry):
        found = to_rows(1, g)
        for c in range(3):
            rows[c, pl.ds(pl.multiple_of(g * 8, 8), 8), :] = found[8 * c:8 * c + 8]
        return carry

    lax.fori_loop(0, GROUPS, second_rows, 0, unroll=8)

    for side in range(2):
        wanted = send_ref[:, 128 * side:128 * side + 128]
        which = jnp.broadcast_to(lax.bitwise_and(wanted, 127), (8, 128))
        tile = lax.shift_right_logical(wanted, 7)
        for c in range(3):
            total = jnp.zeros((8, 128), F32)
            for v in range(8):
                found = jnp.take_along_axis(
                    rows[c, 8 * v:8 * v + 8, :], which, axis=1, mode="promise_in_bounds"
                )
                total = total + jnp.where(sub + 8 * v == tile, found, 0.0)
            ms[side, c:c + 1, :] = jnp.sum(total, axis=0, keepdims=True)
    go_left = remote(ms.at[0], mr.at[1], gs.at[0], gr.at[0], (left, s))
    go_right = remote(ms.at[1], mr.at[0], gs.at[1], gr.at[1], (right, s))
    go_left.start()
    go_right.start()
    go_left.wait_recv()
    go_right.wait_recv()
    for v in range(8):
        source = source_ref[8 * v:8 * v + 8, :]
        which = lax.bitwise_and(source, 127)
        for c in range(3):
            at_left, at_right = (
                jnp.take_along_axis(
                    jnp.broadcast_to(mr[side, c:c + 1, :], (8, 128)), which, axis=1,
                    mode="promise_in_bounds",
                )
                for side in range(2)
            )
            kept = rows[c, 8 * v:8 * v + 8, :]
            rows[c, 8 * v:8 * v + 8, :] = jnp.where(
                source < 8192, kept, jnp.where(source < 8320, at_left, at_right)
            )

    def third_pass(g, carry):
        to_grid(0, g)
        return carry

    lax.fori_loop(0, GROUPS, third_pass, 0, unroll=8)
    sum_bricks(tiles_a)
    send_halo(0)
    run(NZ, lambda d: far_copy(s2b, r2b, b2s, b2r, d).wait_recv())
    nodes_a = by_node(r2b[...], placed)
    for copy in halo(0):
        copy.wait_recv()
    correct(smooth(0), nodes_a[64:128], nodes_a[0:64], tiles_a)

    def last_rows(g, carry):
        found = to_rows(0, g)
        for i in range(8):
            at = pl.ds(pl.multiple_of((g * 8 + i) * TILE, TILE), TILE)
            for c in range(3):
                out_ref[c:c + 1, at] = found[8 * c + i:8 * c + i + 1]
        return carry

    lax.fori_loop(0, GROUPS, last_rows, 0, unroll=8)

    run(NXC, lambda d: near_copy(s1a, r1a, a1s, a1r, d).wait_send())
    run(NXC, lambda d: near_copy(s1b, r1b, b1s, b1r, d).wait_send())
    run(NZ, lambda d: far_copy(s2a, r2a, a2s, a2r, d).wait_send())
    run(NZ, lambda d: far_copy(s2b, r2b, b2s, b2r, d).wait_send())
    for copy in halo(1) + halo(0) + (go_left, go_right):
        copy.wait_send()


def per_device(
    adjoint_end, positions, tile_brick, tile_fill, send_rows, source_rows,
    ckpt_mass, ckpt_velocity, ckpt_target, ckpt_brick, gripper_axis,
):
    hbm = pl.BlockSpec(memory_space=pltpu.HBM)
    dma = pltpu.SemaphoreType.DMA
    return pl.pallas_call(
        kernel,
        out_shape=jax.ShapeDtypeStruct((3, TILES * TILE), F32),
        in_specs=[hbm] * 11,
        out_specs=pl.BlockSpec(memory_space=pltpu.VMEM),
        scratch_shapes=[
            pltpu.VMEM((3, TILES * TILE), F32),
            pltpu.VMEM((3, 2, TILES * TILE), F32),
            pltpu.VMEM((2, TILES), jnp.int32),
            pltpu.SMEM((1, TILES), jnp.int32),
            pltpu.VMEM((1, 256), jnp.int32),
            pltpu.VMEM((TILES, TILE), jnp.int32),
            pltpu.VMEM((128, 128), F32),
            pltpu.VMEM((128, 384), F32),
            pltpu.VMEM((1, 128), jnp.int32),
            pltpu.VMEM((1, 128), jnp.int32),
            pltpu.SMEM((1, 3), F32),
            dma((11,)),
            pltpu.VMEM((2, TILES, 64, 256), BF16),
            pltpu.VMEM((3, TILES, TILE), F32),
            pltpu.VMEM((3, TILES, 128), F32),
            pltpu.VMEM((192, 128), F32),
            pltpu.VMEM((192, 128), F32),
            pltpu.VMEM((6, TILES, 128), F32),
            pltpu.VMEM((NXC * BLOCK, 128), F32),
            pltpu.VMEM((NXC * BLOCK, 128), F32),
            pltpu.VMEM((NXC * BLOCK, 128), F32),
            pltpu.VMEM((NXC * BLOCK, 128), F32),
            pltpu.VMEM((NZ, 17, 128), F32),
            pltpu.VMEM((NZ, 17, 128), F32),
            pltpu.VMEM((NZ, 16, 128), F32),
            pltpu.VMEM((NZ, 16, 128), F32),
            pltpu.VMEM((2, 2, 48, 128), F32),
            pltpu.VMEM((2, 2, 48, 128), F32),
            pltpu.VMEM((2, 2, 12, 4, 128), F32),
            pltpu.VMEM((2, 2, 12, 4, 128), F32),
            pltpu.VMEM((2, 3, 128), F32),
            pltpu.VMEM((2, 3, 128), F32),
            dma((NXC,)), dma((NXC,)), dma((NXC,)), dma((NXC,)),
            dma((NZ,)), dma((NZ,)), dma((NZ,)), dma((NZ,)),
            dma((2, 4)), dma((2, 4)), dma((2,)), dma((2,)),
        ],
        compiler_params=pltpu.CompilerParams(
            collective_id=0, has_side_effects=True, vmem_limit_bytes=60 * 1024 * 1024
        ),
        cost_estimate=pl.CostEstimate(
            flops=200_000_000, bytes_accessed=1_000_000, transcendentals=0
        ),
        name="substeps",
    )(
        adjoint_end, jnp.swapaxes(positions, 0, 1), tile_brick, tile_fill.reshape(1, TILES), send_rows,
        source_rows.reshape(TILES, TILE), ckpt_mass, ckpt_velocity,
        ckpt_target.reshape(1, 128), ckpt_brick.reshape(1, 128), gripper_axis.reshape(1, 3),
    )


def solution(mesh):
    return jax.shard_map(
        per_device,
        mesh=mesh,
        in_specs=(
            P(None, ("brick", "slab")),
            P(None, None, ("brick", "slab")),
            P(None, ("brick", "slab")),
            P(("brick", "slab")),
            P(("brick", "slab"), None),
            P(("brick", "slab")),
            P(("brick", "slab"), None),
            P(("brick", "slab"), None),
            P(("brick", "slab")),
            P(("brick", "slab")),
            P(),
        ),
        out_specs=P(None, ("brick", "slab")),
        check_vma=False,
    )
```

```python
import jax
import jax.numpy as jnp
from jax import lax
from jax.experimental import pallas as pl
from jax.experimental.pallas import tpu as pltpu
from jax.sharding import PartitionSpec as P

TILE = 128
TILES = 64
GROUPS = 8
NZ = 16
NXC = 8
N_BRICK = 128
N_SLAB = 4
BLOCK = 40

diffusion = 0.15
F32 = jnp.float32
BF16 = jnp.bfloat16
MESH = pl.DeviceIdType.MESH


def contract_last(left, right):
    return lax.dot_general(left, right, (((1,), (1,)), ((), ())), preferred_element_type=F32)


def contract_first(left, right):
    return lax.dot_general(left, right, (((0,), (0,)), ((), ())), preferred_element_type=F32)


def split(value):
    high = value.astype(BF16)
    low = (value - high.astype(F32)).astype(BF16)
    return high, low


def iota(shape, dim):
    return lax.broadcasted_iota(jnp.int32, shape, dim)


def bspline(offset):
    magnitude = jnp.abs(offset)
    inner = 0.75 - offset * offset
    tail = 1.5 - magnitude
    outer = 0.5 * tail * tail
    return jnp.where(magnitude < 0.5, inner, jnp.where(magnitude < 1.5, outer, 0.0))


def kernel(
    adj_hbm, pos_hbm, tile_hbm, fill_hbm, send_hbm, source_hbm, mass_hbm, vel_hbm,
    target_hbm, brick_hbm, axis_hbm, out_ref,
    adj_ref, pos_ref, tile_ref, fill_ref, send_ref, source_ref, mass_ref, vel_ref,
    target_ref, brick_ref, axis_ref, load_sem,
    weights, rows, per_tile, grid, xsum, ext,
    s1a, r1a, s1b, r1b, s2a, r2a, s2b, r2b,
    xs, xr, ys, yr, ms, mr,
    a1s, a1r, b1s, b1r, a2s, a2r, b2s, b2r, hs, hr, gs, gr,
):
    b = lax.axis_index("brick")
    s = lax.axis_index("slab")
    z = lax.div(b, NXC)
    xc = lax.rem(b, NXC)
    left = lax.rem(b + N_BRICK - 1, N_BRICK)
    right = lax.rem(b + 1, N_BRICK)
    down = lax.rem(s + N_SLAB - 1, N_SLAB)
    up = lax.rem(s + 1, N_SLAB)

    def near(d):
        return lax.rem(xc + d, NXC)

    def far(d):
        turn = lax.div(d, 2) * (1 - 2 * lax.rem(d, 2))
        return lax.rem(z + NZ + NZ // 2 + turn, NZ)

    barrier = pltpu.get_barrier_semaphore()

    def greet_near(d, carry):
        pl.semaphore_signal(barrier, inc=1, device_id=(z * NXC + near(d), s), device_id_type=MESH)
        return carry

    def greet_far(d, carry):
        pl.semaphore_signal(barrier, inc=1, device_id=(far(d) * NXC + xc, s), device_id_type=MESH)
        return carry

    lax.fori_loop(1, NZ, greet_far, 0)
    lax.fori_loop(1, NXC, greet_near, 0)
    for who in ((left, s), (right, s), (b, down), (b, up)):
        pl.semaphore_signal(barrier, inc=1, device_id=who, device_id_type=MESH)

    loads = [
        pltpu.make_async_copy(src, dst, load_sem.at[i])
        for i, (src, dst) in enumerate((
            (axis_hbm, axis_ref), (vel_hbm, vel_ref), (mass_hbm, mass_ref),
            (target_hbm, target_ref), (brick_hbm, brick_ref), (adj_hbm, adj_ref),
            (pos_hbm, pos_ref), (fill_hbm, fill_ref), (tile_hbm, tile_ref),
            (send_hbm, send_ref), (source_hbm, source_ref),
        ))
    ]
    for load in loads:
        load.start()
    for load in loads[0:5]:
        load.wait()

    def remote(src, dst, send, recv, who):
        return pltpu.make_async_remote_copy(
            src_ref=src, dst_ref=dst, send_sem=send, recv_sem=recv, device_id=who,
            device_id_type=MESH,
        )

    def near_copy(src, dst, send, recv, d):
        to = near(d)
        return remote(
            src.at[pl.ds(pl.multiple_of(to * BLOCK, 8), BLOCK)],
            dst.at[pl.ds(pl.multiple_of(xc * BLOCK, 8), BLOCK)],
            send.at[d], recv.at[d], (z * NXC + to, s),
        )

    def far_copy(src, dst, send, recv, d):
        to = far(d)
        return remote(src.at[to], dst.at[z], send.at[d], recv.at[d], (to * NXC + xc, s))

    def run(count, act):
        def body(d, carry):
            act(d)
            return carry

        lax.fori_loop(1, count, body, 0)

    lane = iota((8, 128), 1)
    axis = [jnp.full((1, 128), axis_ref[0, c], F32) for c in range(3)]
    length = jnp.sqrt(axis[0] * axis[0] + axis[1] * axis[1] + axis[2] * axis[2])
    normal = [a / length for a in axis]
    lane_q = iota((128, 128), 1)
    v0 = vel_ref[:, 0:128]
    v1 = vel_ref[:, 128:256]
    v2 = vel_ref[:, 256:384]
    speed_first = normal[0] * v0 + normal[1] * pltpu.roll(v0, 64, 1) + normal[2] * v1
    speed_second = normal[0] * v1 + normal[1] * pltpu.roll(v2, 64, 1) + normal[2] * v2
    speed = jnp.where(lane_q < 64, speed_first, speed_second)
    contact = jnp.where(speed < 0.0, 1.0, 0.0)
    mass_turned = pltpu.roll(mass_ref[...], 64, 1)
    packed_a = jnp.where(lane_q < 64, mass_turned, contact)
    packed_b = jnp.where(lane_q < 64, contact, mass_turned)
    both = jnp.concatenate([packed_a, packed_b], axis=1)
    high, low = split(both)
    target = target_ref[...]
    slot = lax.bitwise_and(target, 1)
    peer = lax.shift_right_logical(target, 1)
    peer_near = lax.bitwise_and(peer, NXC - 1)
    within = slot * NZ + lax.shift_right_logical(peer, 3)
    place = peer_near * 32 + within
    chosen = jnp.where(iota((256, 128), 0) == place, 1.0, 0.0).astype(BF16)
    packed = jnp.dot(
        jnp.concatenate([chosen, chosen], axis=1), jnp.concatenate([high, low], axis=0),
        preferred_element_type=F32,
    )
    index_left = jnp.where(
        iota((16, 128), 0) == peer_near, (brick_ref[...] + 1).astype(F32), 0.0
    ).astype(BF16)
    index_right = jnp.where(iota((128, 128), 0) == within, 1.0, 0.0).astype(BF16)
    index_out = contract_last(index_left, index_right)
    for i in range(NXC):
        s1a[BLOCK * i:BLOCK * i + 32, :] = packed[32 * i:32 * i + 32, 0:128]
        s1a[BLOCK * i + 32:BLOCK * i + 40, :] = jnp.broadcast_to(index_out[i:i + 1], (8, 128))
        s1b[BLOCK * i:BLOCK * i + 32, :] = packed[32 * i:32 * i + 32, 128:256]
        s1b[BLOCK * i + 32:BLOCK * i + 40, :] = jnp.zeros((8, 128), F32)

    pl.semaphore_wait(barrier, NXC - 1 + NZ - 1 + 4)
    run(NXC, lambda d: near_copy(s1a, r1a, a1s, a1r, d).start())
    own = pl.ds(pl.multiple_of(xc * BLOCK, 8), BLOCK)
    r1a[own] = s1a[own]
    r1b[own] = s1b[own]

    for load in loads[5:11]:
        load.wait()

    def spread(t, carry):
        block = adj_ref[:, pl.ds(pl.multiple_of(t * TILE, TILE), TILE)]
        for c in range(3):
            rows[c, pl.ds(t, 1), :] = block[c:c + 1]
        return carry

    lax.fori_loop(0, TILES, spread, 0, unroll=8)

    sub = iota((8, 128), 0)
    node_x = lax.bitwise_and(sub, 3).astype(F32)
    node_y = lax.shift_right_logical(sub, 2).astype(F32)
    row48 = lax.bitwise_and(iota((48, 128), 0), 7)

    def build(k, g):
        for i in range(8):
            t = g * 8 + i
            at = pl.ds(pl.multiple_of(t * TILE, TILE), TILE)
            pz, py, px = (
                jnp.broadcast_to(pos_ref[c, k:k + 1, at], (8, 128)) for c in range(3)
            )
            pz = jnp.where(lane < fill_ref[0, t], pz, 100.0)
            wx = bspline(px - node_x)
            wz = bspline(pz - node_x)
            xy = [bspline(py - node_y) * wx, bspline(py - (node_y + 2.0)) * wx]
            value = jnp.concatenate(
                [jnp.broadcast_to(wz[n:n + 1], (8, 128)) * xy[h] for n in range(4) for h in range(2)],
                axis=0,
            )
            high, low = split(value)
            weights[k, t, :, 0:128] = high
            weights[k, t, :, 128:256] = low

    def to_grid(k, g):
        at = pl.ds(pl.multiple_of(g * 8, 8), 8)
        parts = [rows[c, at, :] for c in range(3)]
        value = jnp.concatenate(parts, axis=0)
        high = value.astype(BF16).astype(F32)
        value = jnp.concatenate([high, value - high], axis=0)
        lhs = jnp.concatenate(
            [jnp.where(row48 == i, value, 0.0).astype(BF16) for i in range(8)], axis=1
        )
        rhs = jnp.concatenate(
            [
                jnp.concatenate(
                    [weights[k, g * 8 + i, :, 0:128], weights[k, g * 8 + i, :, 128:256]], axis=0
                )
                for i in range(8)
            ],
            axis=1,
        )
        found = contract_last(lhs, rhs)
        found = found[0:24] + found[24:48]
        for c in range(3):
            per_tile[c, at, :] = found[8 * c:8 * c + 8]

    def table(k):
        line = jnp.broadcast_to(tile_ref[k:k + 1, :].astype(F32), (TILES, TILES))
        mine = iota((TILES, TILES), 0) == iota((TILES, TILES), 1)
        column = jnp.sum(jnp.where(mine, line, 0.0), axis=1, keepdims=True)
        return jnp.where(iota((TILES, 128), 1).astype(F32) == column, 1.0, 0.0).astype(BF16)

    def sum_bricks(tiles):
        value = jnp.concatenate([per_tile[c] for c in range(3)], axis=1)
        high, low = split(value)
        found = contract_first(
            jnp.concatenate([high, low], axis=0), jnp.concatenate([tiles, tiles], axis=0)
        )
        for c in range(3):
            grid[64 * c:64 * c + 64, :] = (
                found[128 * c:128 * c + 64] + found[128 * c + 64:128 * c + 128]
            )

    def halo(k):
        x_high = remote(xs.at[k, 0], xr.at[k, 0], hs.at[k, 0], hr.at[k, 0], (right, s))
        x_low = remote(xs.at[k, 1], xr.at[k, 1], hs.at[k, 1], hr.at[k, 1], (left, s))
        y_high = remote(ys.at[k, 0], yr.at[k, 0], hs.at[k, 2], hr.at[k, 2], (b, up))
        y_low = remote(ys.at[k, 1], yr.at[k, 1], hs.at[k, 3], hr.at[k, 3], (b, down))
        return x_high, x_low, y_high, y_low

    brick_lane = iota((1, 128), 1)
    lane_x = lax.bitwise_and(brick_lane, 7)
    lane_y = lax.bitwise_and(lax.shift_right_logical(brick_lane, 3), 3)
    lane_z = lax.shift_right_logical(brick_lane, 5)
    lane_y3 = lane_y.reshape(1, 1, 128)

    def send_halo(k):
        for side in range(2):
            plane = grid[pl.ds(3 - 3 * side, 48, stride=4), :]
            found = jnp.zeros((8, 128), F32)
            for i in range(6):
                part = plane[8 * i:8 * i + 8]
                turn = (i - 7 + 7 * side) % 128
                part = pltpu.roll(part, turn, 1) if turn else part
                found = jnp.where(lane_x == i, part, found)
            xs[k, side] = found
        cells = grid[...].reshape(12, 16, 128)
        for side in range(2):
            plane = cells[:, 12 - 12 * side:16 - 12 * side]
            found = plane[0:3]
            found = pltpu.roll(found, 104, 2) if side == 0 else found
            for i in range(1, 4):
                part = plane[3 * i:3 * i + 3]
                turn = (8 * i - 24 + 24 * side) % 128
                part = pltpu.roll(part, turn, 2) if turn else part
                found = jnp.where(lane_y3 == i, part, found)
            ys[k, side] = found
        for copy in halo(k):
            copy.start()

    has_left = jnp.where(b > 0, 1.0, 0.0)
    has_right = jnp.where(b < N_BRICK - 1, 1.0, 0.0)
    has_down = jnp.where(s > 0, 1.0, 0.0)
    has_up = jnp.where(s < N_SLAB - 1, 1.0, 0.0)

    def smooth(k):
        planes = [grid[pl.ds(j, 48, stride=4), :] for j in range(4)]
        came = xr[k, 0] * has_left
        came = jnp.concatenate(
            [came] + [pltpu.roll(came, 128 - i, 1) for i in range(1, 6)], axis=0
        )
        before = jnp.where(lane_x == 0, came, pltpu.roll(planes[3], 1, 1))
        came = xr[k, 1] * has_right
        came = jnp.concatenate([pltpu.roll(came, 7 - i, 1) for i in range(6)], axis=0)
        after = jnp.where(lane_x == 7, came, pltpu.roll(planes[0], 127, 1))
        line = [before] + planes + [after]
        for j in range(4):
            xsum[pl.ds(j, 48, stride=4), :] = line[j] + line[j + 2]
        cells = grid[...].reshape(12, 16, 128)
        came = yr[k, 0] * has_down
        low = jnp.concatenate(
            [came] + [pltpu.roll(came, 128 - 8 * i, 2) for i in range(1, 4)], axis=0
        )
        came = yr[k, 1] * has_up
        high = jnp.concatenate(
            [pltpu.roll(came, 24 - 8 * i, 2) for i in range(3)] + [came], axis=0
        )
        below = jnp.where(lane_y3 == 0, low, pltpu.roll(cells[:, 12:16], 8, 2))
        above = jnp.where(lane_y3 == 3, high, pltpu.roll(cells[:, 0:4], 120, 2))
        ysum = jnp.concatenate([cells[:, 4:16], above], axis=1) + jnp.concatenate(
            [below, cells[:, 0:12]], axis=1
        )
        out = []
        for c in range(3):
            base = grid[64 * c:64 * c + 64, :]
            last = jnp.where(lane_z == 0, 0.0, pltpu.roll(base[48:64], 32, 1))
            first = jnp.where(lane_z == 3, 0.0, pltpu.roll(base[0:16], 96, 1))
            zsum = jnp.concatenate([base[16:64], first], axis=0) + jnp.concatenate(
                [last, base[0:48]], axis=0
            )
            beside = (
                xsum[64 * c:64 * c + 64, :] + ysum[4 * c:4 * c + 4].reshape(64, 128) + zsum
            )
            out.append(base + diffusion * (beside - 6.0 * base))
        return out

    def relay(src, dst, i):
        dst[i, 0:8, :] = src[pl.ds(i, 8, stride=BLOCK), :]
        dst[i, 8:16, :] = src[pl.ds(NZ + i, 8, stride=BLOCK), :]

    def by_node(got, place):
        value = got.reshape(256, 128)
        high, low = split(value)
        return contract_first(
            jnp.concatenate([high, low], axis=0), jnp.concatenate([place, place], axis=0)
        )

    def correct(cells, mass, touch, tiles):
        project = normal[0] * cells[0] + normal[1] * cells[1] + normal[2] * cells[2]
        scaled = [(cells[c] - touch * normal[c] * project) / mass for c in range(3)]
        highs, lows = zip(*(split(value) for value in scaled))
        stack = jnp.concatenate(
            [part for half in (highs, lows) for value in half for part in (value, value)], axis=0
        )
        found = contract_last(tiles, stack)
        for i in range(6):
            ext[i] = found[:, 128 * i:128 * i + 128]

    pair_of = lax.bitwise_and(iota((8, 128), 0), 7) * 64
    lane_pair = lax.bitwise_and(lane, 64)

    def to_rows(k, g):
        at = pl.ds(pl.multiple_of(g * 8, 8), 8)
        parts = [ext[i, at, :] for i in range(6)]
        lhs = jnp.concatenate(
            [
                jnp.concatenate(
                    [jnp.where(pair_of == lane_pair + 128 * j, part, 0.0) for part in parts], axis=0
                ).astype(BF16)
                for j in range(4)
            ],
            axis=1,
        )
        rhs = jnp.concatenate([weights[k, g * 8 + i] for i in range(8)], axis=0)
        found = jnp.dot(lhs, rhs, preferred_element_type=F32)
        return found[0:24, 0:128] + found[24:48, 0:128] + found[0:24, 128:256]

    def first_pass(g, carry):
        build(1, g)
        to_grid(1, g)
        return carry

    lax.fori_loop(0, GROUPS, first_pass, 0, unroll=2)
    tiles_b = table(1)
    sum_bricks(tiles_b)
    send_halo(1)

    run(NXC, lambda d: near_copy(s1a, r1a, a1s, a1r, d).wait_recv())
    index_in = r1a[pl.ds(32, 8, stride=BLOCK), :]
    index_two = jnp.concatenate([index_in, pltpu.roll(index_in, 112, 1)], axis=0)
    index_two = jnp.where(iota((16, 128), 1) < NZ, index_two, 0.0).astype(BF16)
    pick = jnp.where(iota((NZ, 128), 0) == iota((NZ, 128), 1), 1.0, 0.0).astype(BF16)
    index_far = contract_last(
        pick, jnp.concatenate([index_two, jnp.zeros((112, 128), BF16)], axis=0)
    )
    for i in range(NZ):
        s2a[i, 16:17, :] = index_far[i:i + 1]

    def leave_a(d):
        relay(r1a, s2a, far(d))
        far_copy(s2a, r2a, a2s, a2r, d).start()

    run(NZ, leave_a)
    relay(r1a, s2a, z)
    r2a[z] = s2a[z]
    run(NXC, lambda d: near_copy(s1b, r1b, b1s, b1r, d).start())

    def second_weights(g, carry):
        build(0, g)
        return carry

    lax.fori_loop(0, GROUPS, second_weights, 0, unroll=2)
    tiles_a = table(0)

    for copy in halo(1):
        copy.wait_recv()
    cells = smooth(1)


    run(NZ, lambda d: far_copy(s2a, r2a, a2s, a2r, d).wait_recv())
    index_row = jnp.concatenate([r2a[i, 16:17, :] for i in range(NZ)], axis=0)
    spread_index = jnp.concatenate(
        [jnp.broadcast_to(index_row[i:i + 1], (16, 128)) for i in range(NZ)], axis=0
    )
    mine = lax.bitwise_and(iota((256, 128), 0), 15) == iota((256, 128), 1)
    column = jnp.sum(jnp.where(mine, spread_index, 0.0), axis=1, keepdims=True) - 1.0
    placed = jnp.where(iota((256, 128), 1).astype(F32) == column, 1.0, 0.0).astype(BF16)
    nodes_b = by_node(jnp.concatenate([r2a[i, 0:16, :] for i in range(NZ)], axis=0), placed)
    correct(cells, nodes_b[0:64], nodes_b[64:128], tiles_b)

    def second_rows(g, carry):
        found = to_rows(1, g)
        for c in range(3):
            rows[c, pl.ds(pl.multiple_of(g * 8, 8), 8), :] = found[8 * c:8 * c + 8]
        return carry

    lax.fori_loop(0, GROUPS, second_rows, 0, unroll=8)

    for side in range(2):
        wanted = send_ref[:, 128 * side:128 * side + 128]
        which = jnp.broadcast_to(lax.bitwise_and(wanted, 127), (8, 128))
        tile = lax.shift_right_logical(wanted, 7)
        for c in range(3):
            total = jnp.zeros((8, 128), F32)
            for v in range(8):
                found = jnp.take_along_axis(
                    rows[c, 8 * v:8 * v + 8, :], which, axis=1, mode="promise_in_bounds"
                )
                total = total + jnp.where(sub + 8 * v == tile, found, 0.0)
            ms[side, c:c + 1, :] = jnp.sum(total, axis=0, keepdims=True)
    go_left = remote(ms.at[0], mr.at[1], gs.at[0], gr.at[0], (left, s))
    go_right = remote(ms.at[1], mr.at[0], gs.at[1], gr.at[1], (right, s))
    go_left.start()
    go_right.start()

    run(NXC, lambda d: near_copy(s1b, r1b, b1s, b1r, d).wait_recv())

    def leave_b(d):
        relay(r1b, s2b, far(d))
        far_copy(s2b, r2b, b2s, b2r, d).start()

    run(NZ, leave_b)
    relay(r1b, s2b, z)
    r2b[z] = s2b[z]

    go_left.wait_recv()
    go_right.wait_recv()
    for v in range(8):
        source = source_ref[8 * v:8 * v + 8, :]
        which = lax.bitwise_and(source, 127)
        for c in range(3):
            at_left, at_right = (
                jnp.take_along_axis(
                    jnp.broadcast_to(mr[side, c:c + 1, :], (8, 128)), which, axis=1,
                    mode="promise_in_bounds",
                )
                for side in range(2)
            )
            kept = rows[c, 8 * v:8 * v + 8, :]
            rows[c, 8 * v:8 * v + 8, :] = jnp.where(
                source < 8192, kept, jnp.where(source < 8320, at_left, at_right)
            )

    def third_pass(g, carry):
        to_grid(0, g)
        return carry

    lax.fori_loop(0, GROUPS, third_pass, 0, unroll=8)
    sum_bricks(tiles_a)
    send_halo(0)
    run(NZ, lambda d: far_copy(s2b, r2b, b2s, b2r, d).wait_recv())
    nodes_a = by_node(r2b[...], placed)
    for copy in halo(0):
        copy.wait_recv()
    correct(smooth(0), nodes_a[64:128], nodes_a[0:64], tiles_a)

    def last_rows(g, carry):
        found = to_rows(0, g)
        for i in range(8):
            at = pl.ds(pl.multiple_of((g * 8 + i) * TILE, TILE), TILE)
            for c in range(3):
                out_ref[c:c + 1, at] = found[8 * c + i:8 * c + i + 1]
        return carry

    lax.fori_loop(0, GROUPS, last_rows, 0, unroll=8)

    run(NXC, lambda d: near_copy(s1a, r1a, a1s, a1r, d).wait_send())
    run(NXC, lambda d: near_copy(s1b, r1b, b1s, b1r, d).wait_send())
    run(NZ, lambda d: far_copy(s2a, r2a, a2s, a2r, d).wait_send())
    run(NZ, lambda d: far_copy(s2b, r2b, b2s, b2r, d).wait_send())
    for copy in halo(1) + halo(0) + (go_left, go_right):
        copy.wait_send()


def per_device(
    adjoint_end, positions, tile_brick, tile_fill, send_rows, source_rows,
    ckpt_mass, ckpt_velocity, ckpt_target, ckpt_brick, gripper_axis,
):
    hbm = pl.BlockSpec(memory_space=pltpu.HBM)
    dma = pltpu.SemaphoreType.DMA
    return pl.pallas_call(
        kernel,
        out_shape=pltpu.VMEM((3, TILES * TILE), F32),
        in_specs=[hbm] * 11,
        out_specs=pl.BlockSpec(memory_space=pltpu.VMEM),
        scratch_shapes=[
            pltpu.VMEM((3, TILES * TILE), F32),
            pltpu.VMEM((3, 2, TILES * TILE), F32),
            pltpu.VMEM((2, TILES), jnp.int32),
            pltpu.SMEM((1, TILES), jnp.int32),
            pltpu.VMEM((1, 256), jnp.int32),
            pltpu.VMEM((TILES, TILE), jnp.int32),
            pltpu.VMEM((128, 128), F32),
            pltpu.VMEM((128, 384), F32),
            pltpu.VMEM((1, 128), jnp.int32),
            pltpu.VMEM((1, 128), jnp.int32),
            pltpu.SMEM((1, 3), F32),
            dma((11,)),
            pltpu.VMEM((2, TILES, 64, 256), BF16),
            pltpu.VMEM((3, TILES, TILE), F32),
            pltpu.VMEM((3, TILES, 128), F32),
            pltpu.VMEM((192, 128), F32),
            pltpu.VMEM((192, 128), F32),
            pltpu.VMEM((6, TILES, 128), F32),
            pltpu.VMEM((NXC * BLOCK, 128), F32),
            pltpu.VMEM((NXC * BLOCK, 128), F32),
            pltpu.VMEM((NXC * BLOCK, 128), F32),
            pltpu.VMEM((NXC * BLOCK, 128), F32),
            pltpu.VMEM((NZ, 17, 128), F32),
            pltpu.VMEM((NZ, 17, 128), F32),
            pltpu.VMEM((NZ, 16, 128), F32),
            pltpu.VMEM((NZ, 16, 128), F32),
            pltpu.VMEM((2, 2, 8, 128), F32),
            pltpu.VMEM((2, 2, 8, 128), F32),
            pltpu.VMEM((2, 2, 3, 4, 128), F32),
            pltpu.VMEM((2, 2, 3, 4, 128), F32),
            pltpu.VMEM((2, 3, 128), F32),
            pltpu.VMEM((2, 3, 128), F32),
            dma((NXC,)), dma((NXC,)), dma((NXC,)), dma((NXC,)),
            dma((NZ,)), dma((NZ,)), dma((NZ,)), dma((NZ,)),
            dma((2, 4)), dma((2, 4)), dma((2,)), dma((2,)),
        ],
        compiler_params=pltpu.CompilerParams(
            collective_id=0, has_side_effects=True, vmem_limit_bytes=60 * 1024 * 1024
        ),
        cost_estimate=pl.CostEstimate(
            flops=200_000_000, bytes_accessed=1_000_000, transcendentals=0
        ),
        name="substeps",
    )(
        adjoint_end, jnp.swapaxes(positions, 0, 1), tile_brick, tile_fill.reshape(1, TILES), send_rows,
        source_rows.reshape(TILES, TILE), ckpt_mass, ckpt_velocity,
        ckpt_target.reshape(1, 128), ckpt_brick.reshape(1, 128), gripper_axis.reshape(1, 3),
    )


def solution(mesh):
    return jax.shard_map(
        per_device,
        mesh=mesh,
        in_specs=(
            P(None, ("brick", "slab")),
            P(None, None, ("brick", "slab")),
            P(None, ("brick", "slab")),
            P(("brick", "slab")),
            P(("brick", "slab"), None),
            P(("brick", "slab")),
            P(("brick", "slab"), None),
            P(("brick", "slab"), None),
            P(("brick", "slab")),
            P(("brick", "slab")),
            P(),
        ),
        out_specs=P(None, ("brick", "slab")),
        check_vma=False,
    )
```

```python
import jax
import jax.numpy as jnp
from jax import lax
from jax.experimental import pallas as pl
from jax.experimental.pallas import tpu as pltpu
from jax.sharding import PartitionSpec as P

TILE = 128
TILES = 64
GROUPS = 8
NZ = 16
NXC = 8
N_BRICK = 128
N_SLAB = 4

diffusion = 0.15
F32 = jnp.float32
BF16 = jnp.bfloat16
MESH = pl.DeviceIdType.MESH


def contract_last(left, right):
    return lax.dot_general(left, right, (((1,), (1,)), ((), ())), preferred_element_type=F32)


def contract_first(left, right):
    return lax.dot_general(left, right, (((0,), (0,)), ((), ())), preferred_element_type=F32)


def split(value):
    high = value.astype(BF16)
    low = (value - high.astype(F32)).astype(BF16)
    return high, low


def iota(shape, dim):
    return lax.broadcasted_iota(jnp.int32, shape, dim)


def bspline(offset):
    magnitude = jnp.abs(offset)
    inner = 0.75 - offset * offset
    tail = 1.5 - magnitude
    outer = 0.5 * tail * tail
    return jnp.where(magnitude < 0.5, inner, jnp.where(magnitude < 1.5, outer, 0.0))


def kernel(
    adj_hbm, pos_hbm, tile_hbm, fill_hbm, send_hbm, source_hbm, mass_hbm, vel_hbm,
    target_hbm, brick_hbm, axis_hbm, out_ref,
    adj_ref, pos_ref, tile_ref, fill_ref, send_ref, source_ref, mass_ref, vel_ref,
    target_ref, brick_ref, axis_ref, load_sem,
    weights, rows, per_tile, grid, xsum, ext,
    s1a, r1a, s1b, r1b, s2a, r2a, s2b, r2b,
    xs, xr, ys, yr, ms, mr,
    a1s, a1r, b1s, b1r, a2s, a2r, b2s, b2r, hs, hr, gs, gr,
):
    b = lax.axis_index("brick")
    s = lax.axis_index("slab")
    z = lax.div(b, NXC)
    xc = lax.rem(b, NXC)
    left = lax.rem(b + N_BRICK - 1, N_BRICK)
    right = lax.rem(b + 1, N_BRICK)
    down = lax.rem(s + N_SLAB - 1, N_SLAB)
    up = lax.rem(s + 1, N_SLAB)

    def near(d):
        return lax.rem(xc + (4, 5, 3, 6, 2, 7, 1)[d - 1], NXC)

    def far(d):
        turn = (d // 2) * (1 - 2 * (d % 2))
        return lax.rem(z + NZ + NZ // 2 + turn * (1 - 2 * lax.rem(xc, 2)), NZ)

    barrier = pltpu.get_barrier_semaphore()

    def greet_near(d):
        pl.semaphore_signal(barrier, inc=1, device_id=(z * NXC + near(d), s), device_id_type=MESH)

    def greet_far(d):
        pl.semaphore_signal(barrier, inc=1, device_id=(far(d) * NXC + xc, s), device_id_type=MESH)

    for d in range(1, NZ):
        greet_far(d)
    for d in range(1, NXC):
        greet_near(d)
    for who in ((left, s), (right, s), (b, down), (b, up)):
        pl.semaphore_signal(barrier, inc=1, device_id=who, device_id_type=MESH)

    loads = [
        pltpu.make_async_copy(src, dst, load_sem.at[i])
        for i, (src, dst) in enumerate((
            (axis_hbm, axis_ref), (vel_hbm, vel_ref), (mass_hbm, mass_ref),
            (target_hbm, target_ref), (brick_hbm, brick_ref), (adj_hbm, adj_ref),
            (pos_hbm, pos_ref), (fill_hbm, fill_ref), (tile_hbm, tile_ref),
            (send_hbm, send_ref), (source_hbm, source_ref),
        ))
    ]
    for load in loads:
        load.start()
    for load in loads[0:5]:
        load.wait()

    def remote(src, dst, send, recv, who):
        return pltpu.make_async_remote_copy(
            src_ref=src, dst_ref=dst, send_sem=send, recv_sem=recv, device_id=who,
            device_id_type=MESH,
        )

    def near_copy(src, dst, send, recv, d):
        to = near(d)
        return remote(src.at[to], dst.at[xc], send.at[d], recv.at[d], (z * NXC + to, s))

    def far_copy(src, dst, send, recv, d):
        to = far(d)
        return remote(src.at[to], dst.at[z], send.at[d], recv.at[d], (to * NXC + xc, s))

    def run(count, act):
        for d in range(1, count):
            act(d)

    lane = iota((8, 128), 1)
    axis = [jnp.full((1, 128), axis_ref[0, c], F32) for c in range(3)]
    length = jnp.sqrt(axis[0] * axis[0] + axis[1] * axis[1] + axis[2] * axis[2])
    normal = [a / length for a in axis]
    lane_q = iota((128, 128), 1)
    v0 = vel_ref[:, 0:128]
    v1 = vel_ref[:, 128:256]
    v2 = vel_ref[:, 256:384]
    speed_first = normal[0] * v0 + normal[1] * pltpu.roll(v0, 64, 1) + normal[2] * v1
    speed_second = normal[0] * v1 + normal[1] * pltpu.roll(v2, 64, 1) + normal[2] * v2
    speed = jnp.where(lane_q < 64, speed_first, speed_second)
    contact = jnp.where(speed < 0.0, 1.0, 0.0)
    mass_turned = pltpu.roll(mass_ref[...], 64, 1)
    packed_a = jnp.where(lane_q < 64, mass_turned, contact)
    packed_b = jnp.where(lane_q < 64, contact, mass_turned)
    both = jnp.concatenate([packed_a, packed_b], axis=1)
    high, low = split(both)
    target = target_ref[...]
    slot = lax.bitwise_and(target, 1)
    peer = lax.shift_right_logical(target, 1)
    peer_near = lax.bitwise_and(peer, NXC - 1)
    within = slot * NZ + lax.shift_right_logical(peer, 3)
    place = peer_near * 32 + within
    chosen = jnp.where(iota((256, 128), 0) == place, 1.0, 0.0).astype(BF16)
    packed = jnp.dot(
        jnp.concatenate([chosen, chosen], axis=1), jnp.concatenate([high, low], axis=0),
        preferred_element_type=F32,
    )
    index_left = jnp.where(
        iota((16, 128), 0) == peer_near, (brick_ref[...] + 1).astype(F32), 0.0
    ).astype(BF16)
    index_right = jnp.where(iota((128, 128), 0) == within, 1.0, 0.0).astype(BF16)
    index_out = contract_last(index_left, index_right)
    for i in range(NXC):
        s1a[i, 0:32, :] = packed[32 * i:32 * i + 32, 0:128]
        s1a[i, 32:33, :] = index_out[i:i + 1]
        s1b[i] = packed[32 * i:32 * i + 32, 128:256]

    pl.semaphore_wait(barrier, NXC - 1 + NZ - 1 + 4)
    run(NXC, lambda d: near_copy(s1a, r1a, a1s, a1r, d).start())
    r1a[xc] = s1a[xc]
    r1b[xc] = s1b[xc]

    for load in loads[5:11]:
        load.wait()

    def spread(t, carry):
        block = adj_ref[:, pl.ds(pl.multiple_of(t * TILE, TILE), TILE)]
        for c in range(3):
            rows[c, pl.ds(t, 1), :] = block[c:c + 1]
        return carry

    lax.fori_loop(0, TILES, spread, 0, unroll=8)

    sub = iota((8, 128), 0)
    node_x = lax.bitwise_and(sub, 3).astype(F32)
    node_y = lax.shift_right_logical(sub, 2).astype(F32)
    row48 = lax.bitwise_and(iota((48, 128), 0), 7)

    def build(k, g):
        for i in range(8):
            t = g * 8 + i
            at = pl.ds(pl.multiple_of(t * TILE, TILE), TILE)
            pz, py, px = (
                jnp.broadcast_to(pos_ref[c, k:k + 1, at], (8, 128)) for c in range(3)
            )
            pz = jnp.where(lane < fill_ref[0, t], pz, 100.0)
            wx = bspline(px - node_x)
            wz = bspline(pz - node_x)
            xy = [bspline(py - node_y) * wx, bspline(py - (node_y + 2.0)) * wx]
            value = jnp.concatenate(
                [jnp.broadcast_to(wz[n:n + 1], (8, 128)) * xy[h] for n in range(4) for h in range(2)],
                axis=0,
            )
            high, low = split(value)
            weights[k, t, :, 0:128] = high
            weights[k, t, :, 128:256] = low

    def to_grid(k, g):
        at = pl.ds(pl.multiple_of(g * 8, 8), 8)
        parts = [rows[c, at, :] for c in range(3)]
        value = jnp.concatenate(parts, axis=0)
        high = value.astype(BF16).astype(F32)
        value = jnp.concatenate([high, value - high], axis=0)
        lhs = jnp.concatenate(
            [jnp.where(row48 == i, value, 0.0).astype(BF16) for i in range(8)], axis=1
        )
        rhs = jnp.concatenate(
            [
                jnp.concatenate(
                    [weights[k, g * 8 + i, :, 0:128], weights[k, g * 8 + i, :, 128:256]], axis=0
                )
                for i in range(8)
            ],
            axis=1,
        )
        found = contract_last(lhs, rhs)
        found = found[0:24] + found[24:48]
        for c in range(3):
            per_tile[c, at, :] = found[8 * c:8 * c + 8]

    def table(k):
        line = jnp.broadcast_to(tile_ref[k:k + 1, :].astype(F32), (TILES, TILES))
        mine = iota((TILES, TILES), 0) == iota((TILES, TILES), 1)
        column = jnp.sum(jnp.where(mine, line, 0.0), axis=1, keepdims=True)
        return jnp.where(iota((TILES, 128), 1).astype(F32) == column, 1.0, 0.0).astype(BF16)

    def sum_bricks(tiles):
        value = jnp.concatenate([per_tile[c] for c in range(3)], axis=1)
        high, low = split(value)
        found = contract_first(
            jnp.concatenate([high, low], axis=0), jnp.concatenate([tiles, tiles], axis=0)
        )
        for c in range(3):
            grid[64 * c:64 * c + 64, :] = (
                found[128 * c:128 * c + 64] + found[128 * c + 64:128 * c + 128]
            )

    def halo(k):
        x_high = remote(xs.at[k, 0], xr.at[k, 0], hs.at[k, 0], hr.at[k, 0], (right, s))
        x_low = remote(xs.at[k, 1], xr.at[k, 1], hs.at[k, 1], hr.at[k, 1], (left, s))
        y_high = remote(ys.at[k, 0], yr.at[k, 0], hs.at[k, 2], hr.at[k, 2], (b, up))
        y_low = remote(ys.at[k, 1], yr.at[k, 1], hs.at[k, 3], hr.at[k, 3], (b, down))
        return x_high, x_low, y_high, y_low

    brick_lane = iota((1, 128), 1)
    lane_x = lax.bitwise_and(brick_lane, 7)
    lane_y = lax.bitwise_and(lax.shift_right_logical(brick_lane, 3), 3)
    lane_z = lax.shift_right_logical(brick_lane, 5)
    lane_y3 = lane_y.reshape(1, 1, 128)

    def send_halo(k):
        for side in range(2):
            plane = grid[pl.ds(3 - 3 * side, 48, stride=4), :]
            found = jnp.zeros((8, 128), F32)
            for i in range(6):
                part = plane[8 * i:8 * i + 8]
                turn = (i - 7 + 7 * side) % 128
                part = pltpu.roll(part, turn, 1) if turn else part
                found = jnp.where(lane_x == i, part, found)
            xs[k, side] = found
        cells = grid[...].reshape(12, 16, 128)
        for side in range(2):
            plane = cells[:, 12 - 12 * side:16 - 12 * side]
            found = plane[0:3]
            found = pltpu.roll(found, 104, 2) if side == 0 else found
            for i in range(1, 4):
                part = plane[3 * i:3 * i + 3]
                turn = (8 * i - 24 + 24 * side) % 128
                part = pltpu.roll(part, turn, 2) if turn else part
                found = jnp.where(lane_y3 == i, part, found)
            ys[k, side] = found
        for copy in halo(k):
            copy.start()

    has_left = jnp.where(b > 0, 1.0, 0.0)
    has_right = jnp.where(b < N_BRICK - 1, 1.0, 0.0)
    has_down = jnp.where(s > 0, 1.0, 0.0)
    has_up = jnp.where(s < N_SLAB - 1, 1.0, 0.0)

    def smooth(k):
        planes = [grid[pl.ds(j, 48, stride=4), :] for j in range(4)]
        came = xr[k, 0] * has_left
        came = jnp.concatenate(
            [came] + [pltpu.roll(came, 128 - i, 1) for i in range(1, 6)], axis=0
        )
        before = jnp.where(lane_x == 0, came, pltpu.roll(planes[3], 1, 1))
        came = xr[k, 1] * has_right
        came = jnp.concatenate([pltpu.roll(came, 7 - i, 1) for i in range(6)], axis=0)
        after = jnp.where(lane_x == 7, came, pltpu.roll(planes[0], 127, 1))
        line = [before] + planes + [after]
        for j in range(4):
            xsum[pl.ds(j, 48, stride=4), :] = line[j] + line[j + 2]
        cells = grid[...].reshape(12, 16, 128)
        came = yr[k, 0] * has_down
        low = jnp.concatenate(
            [came] + [pltpu.roll(came, 128 - 8 * i, 2) for i in range(1, 4)], axis=0
        )
        came = yr[k, 1] * has_up
        high = jnp.concatenate(
            [pltpu.roll(came, 24 - 8 * i, 2) for i in range(3)] + [came], axis=0
        )
        below = jnp.where(lane_y3 == 0, low, pltpu.roll(cells[:, 12:16], 8, 2))
        above = jnp.where(lane_y3 == 3, high, pltpu.roll(cells[:, 0:4], 120, 2))
        ysum = jnp.concatenate([cells[:, 4:16], above], axis=1) + jnp.concatenate(
            [below, cells[:, 0:12]], axis=1
        )
        out = []
        for c in range(3):
            base = grid[64 * c:64 * c + 64, :]
            last = jnp.where(lane_z == 0, 0.0, pltpu.roll(base[48:64], 32, 1))
            first = jnp.where(lane_z == 3, 0.0, pltpu.roll(base[0:16], 96, 1))
            zsum = jnp.concatenate([base[16:64], first], axis=0) + jnp.concatenate(
                [last, base[0:48]], axis=0
            )
            beside = (
                xsum[64 * c:64 * c + 64, :] + ysum[4 * c:4 * c + 4].reshape(64, 128) + zsum
            )
            out.append(base + diffusion * (beside - 6.0 * base))
        return out

    def relay(src, dst, i):
        for side in range(2):
            dst[i, 8 * side:8 * side + 8, :] = jnp.concatenate(
                [src[j, pl.ds(NZ * side + i, 1), :] for j in range(NXC)], axis=0
            )

    def by_node(got, place):
        value = got.reshape(256, 128)
        high, low = split(value)
        return contract_first(
            jnp.concatenate([high, low], axis=0), jnp.concatenate([place, place], axis=0)
        )

    def correct(cells, mass, touch, tiles):
        project = normal[0] * cells[0] + normal[1] * cells[1] + normal[2] * cells[2]
        scaled = [(cells[c] - touch * normal[c] * project) / mass for c in range(3)]
        highs, lows = zip(*(split(value) for value in scaled))
        stack = jnp.concatenate(
            [part for half in (highs, lows) for value in half for part in (value, value)], axis=0
        )
        found = contract_last(tiles, stack)
        for i in range(6):
            ext[i] = found[:, 128 * i:128 * i + 128]

    pair_of = lax.bitwise_and(iota((8, 128), 0), 7) * 64
    lane_pair = lax.bitwise_and(lane, 64)

    def to_rows(k, g):
        at = pl.ds(pl.multiple_of(g * 8, 8), 8)
        parts = [ext[i, at, :] for i in range(6)]
        lhs = jnp.concatenate(
            [
                jnp.concatenate(
                    [jnp.where(pair_of == lane_pair + 128 * j, part, 0.0) for part in parts], axis=0
                ).astype(BF16)
                for j in range(4)
            ],
            axis=1,
        )
        rhs = jnp.concatenate([weights[k, g * 8 + i] for i in range(8)], axis=0)
        found = jnp.dot(lhs, rhs, preferred_element_type=F32)
        return found[0:24, 0:128] + found[24:48, 0:128] + found[0:24, 128:256]

    def first_pass(g, carry):
        build(1, g)
        to_grid(1, g)
        return carry

    lax.fori_loop(0, GROUPS, first_pass, 0, unroll=2)
    tiles_b = table(1)
    sum_bricks(tiles_b)
    send_halo(1)

    run(NXC, lambda d: near_copy(s1a, r1a, a1s, a1r, d).wait_recv())
    index_in = jnp.concatenate([r1a[j, 32:33, :] for j in range(NXC)], axis=0)
    index_two = jnp.concatenate([index_in, pltpu.roll(index_in, 112, 1)], axis=0)
    index_two = jnp.where(iota((16, 128), 1) < NZ, index_two, 0.0).astype(BF16)
    pick = jnp.where(iota((NZ, 128), 0) == iota((NZ, 128), 1), 1.0, 0.0).astype(BF16)
    index_far = contract_last(
        pick, jnp.concatenate([index_two, jnp.zeros((112, 128), BF16)], axis=0)
    )
    for i in range(NZ):
        s2a[i, 16:17, :] = index_far[i:i + 1]

    def leave_a(d):
        relay(r1a, s2a, far(d))
        far_copy(s2a, r2a, a2s, a2r, d).start()

    run(NZ, leave_a)
    relay(r1a, s2a, z)
    r2a[z] = s2a[z]
    run(NXC, lambda d: near_copy(s1b, r1b, b1s, b1r, d).start())

    def second_weights(g, carry):
        build(0, g)
        return carry

    lax.fori_loop(0, GROUPS, second_weights, 0, unroll=2)
    tiles_a = table(0)

    for copy in halo(1):
        copy.wait_recv()
    cells = smooth(1)


    run(NZ, lambda d: far_copy(s2a, r2a, a2s, a2r, d).wait_recv())
    index_row = jnp.concatenate([r2a[i, 16:17, :] for i in range(NZ)], axis=0)
    spread_index = jnp.concatenate(
        [jnp.broadcast_to(index_row[i:i + 1], (16, 128)) for i in range(NZ)], axis=0
    )
    mine = lax.bitwise_and(iota((256, 128), 0), 15) == iota((256, 128), 1)
    column = jnp.sum(jnp.where(mine, spread_index, 0.0), axis=1, keepdims=True) - 1.0
    placed = jnp.where(iota((256, 128), 1).astype(F32) == column, 1.0, 0.0).astype(BF16)
    nodes_b = by_node(jnp.concatenate([r2a[i, 0:16, :] for i in range(NZ)], axis=0), placed)
    correct(cells, nodes_b[0:64], nodes_b[64:128], tiles_b)

    def second_rows(g, carry):
        found = to_rows(1, g)
        for c in range(3):
            rows[c, pl.ds(pl.multiple_of(g * 8, 8), 8), :] = found[8 * c:8 * c + 8]
        return carry

    lax.fori_loop(0, GROUPS, second_rows, 0, unroll=8)

    for side in range(2):
        wanted = send_ref[:, 128 * side:128 * side + 128]
        which = jnp.broadcast_to(lax.bitwise_and(wanted, 127), (8, 128))
        tile = lax.shift_right_logical(wanted, 7)
        for c in range(3):
            total = jnp.zeros((8, 128), F32)
            for v in range(8):
                found = jnp.take_along_axis(
                    rows[c, 8 * v:8 * v + 8, :], which, axis=1, mode="promise_in_bounds"
                )
                total = total + jnp.where(sub + 8 * v == tile, found, 0.0)
            ms[side, c:c + 1, :] = jnp.sum(total, axis=0, keepdims=True)
    go_left = remote(ms.at[0], mr.at[1], gs.at[0], gr.at[0], (left, s))
    go_right = remote(ms.at[1], mr.at[0], gs.at[1], gr.at[1], (right, s))
    go_left.start()
    go_right.start()

    run(NXC, lambda d: near_copy(s1b, r1b, b1s, b1r, d).wait_recv())

    def leave_b(d):
        relay(r1b, s2b, far(d))
        far_copy(s2b, r2b, b2s, b2r, d).start()

    run(NZ, leave_b)
    relay(r1b, s2b, z)
    r2b[z] = s2b[z]

    go_left.wait_recv()
    go_right.wait_recv()
    for v in range(8):
        source = source_ref[8 * v:8 * v + 8, :]
        which = lax.bitwise_and(source, 127)
        for c in range(3):
            at_left, at_right = (
                jnp.take_along_axis(
                    jnp.broadcast_to(mr[side, c:c + 1, :], (8, 128)), which, axis=1,
                    mode="promise_in_bounds",
                )
                for side in range(2)
            )
            kept = rows[c, 8 * v:8 * v + 8, :]
            rows[c, 8 * v:8 * v + 8, :] = jnp.where(
                source < 8192, kept, jnp.where(source < 8320, at_left, at_right)
            )

    def third_pass(g, carry):
        to_grid(0, g)
        return carry

    lax.fori_loop(0, GROUPS, third_pass, 0, unroll=8)
    sum_bricks(tiles_a)
    send_halo(0)
    run(NZ, lambda d: far_copy(s2b, r2b, b2s, b2r, d).wait_recv())
    nodes_a = by_node(r2b[...], placed)
    for copy in halo(0):
        copy.wait_recv()
    correct(smooth(0), nodes_a[64:128], nodes_a[0:64], tiles_a)

    def last_rows(g, carry):
        found = to_rows(0, g)
        for i in range(8):
            at = pl.ds(pl.multiple_of((g * 8 + i) * TILE, TILE), TILE)
            for c in range(3):
                out_ref[c:c + 1, at] = found[8 * c + i:8 * c + i + 1]
        return carry

    lax.fori_loop(0, GROUPS, last_rows, 0, unroll=8)

    run(NXC, lambda d: near_copy(s1a, r1a, a1s, a1r, d).wait_send())
    run(NXC, lambda d: near_copy(s1b, r1b, b1s, b1r, d).wait_send())
    run(NZ, lambda d: far_copy(s2a, r2a, a2s, a2r, d).wait_send())
    run(NZ, lambda d: far_copy(s2b, r2b, b2s, b2r, d).wait_send())
    for copy in halo(1) + halo(0) + (go_left, go_right):
        copy.wait_send()


def per_device(
    adjoint_end, positions, tile_brick, tile_fill, send_rows, source_rows,
    ckpt_mass, ckpt_velocity, ckpt_target, ckpt_brick, gripper_axis,
):
    hbm = pl.BlockSpec(memory_space=pltpu.HBM)
    dma = pltpu.SemaphoreType.DMA
    return pl.pallas_call(
        kernel,
        out_shape=pltpu.VMEM((3, TILES * TILE), F32),
        in_specs=[hbm] * 11,
        out_specs=pl.BlockSpec(memory_space=pltpu.VMEM),
        scratch_shapes=[
            pltpu.VMEM((3, TILES * TILE), F32),
            pltpu.VMEM((3, 2, TILES * TILE), F32),
            pltpu.VMEM((2, TILES), jnp.int32),
            pltpu.SMEM((1, TILES), jnp.int32),
            pltpu.VMEM((1, 256), jnp.int32),
            pltpu.VMEM((TILES, TILE), jnp.int32),
            pltpu.VMEM((128, 128), F32),
            pltpu.VMEM((128, 384), F32),
            pltpu.VMEM((1, 128), jnp.int32),
            pltpu.VMEM((1, 128), jnp.int32),
            pltpu.SMEM((1, 3), F32),
            dma((11,)),
            pltpu.VMEM((2, TILES, 64, 256), BF16),
            pltpu.VMEM((3, TILES, TILE), F32),
            pltpu.VMEM((3, TILES, 128), F32),
            pltpu.VMEM((192, 128), F32),
            pltpu.VMEM((192, 128), F32),
            pltpu.VMEM((6, TILES, 128), F32),
            pltpu.VMEM((NXC, 33, 128), F32),
            pltpu.VMEM((NXC, 33, 128), F32),
            pltpu.VMEM((NXC, 32, 128), F32),
            pltpu.VMEM((NXC, 32, 128), F32),
            pltpu.VMEM((NZ, 17, 128), F32),
            pltpu.VMEM((NZ, 17, 128), F32),
            pltpu.VMEM((NZ, 16, 128), F32),
            pltpu.VMEM((NZ, 16, 128), F32),
            pltpu.VMEM((2, 2, 8, 128), F32),
            pltpu.VMEM((2, 2, 8, 128), F32),
            pltpu.VMEM((2, 2, 3, 4, 128), F32),
            pltpu.VMEM((2, 2, 3, 4, 128), F32),
            pltpu.VMEM((2, 3, 128), F32),
            pltpu.VMEM((2, 3, 128), F32),
            dma((NXC,)), dma((NXC,)), dma((NXC,)), dma((NXC,)),
            dma((NZ,)), dma((NZ,)), dma((NZ,)), dma((NZ,)),
            dma((2, 4)), dma((2, 4)), dma((2,)), dma((2,)),
        ],
        compiler_params=pltpu.CompilerParams(
            collective_id=0, has_side_effects=True, vmem_limit_bytes=60 * 1024 * 1024
        ),
        cost_estimate=pl.CostEstimate(
            flops=200_000_000, bytes_accessed=1_000_000, transcendentals=0
        ),
        name="substeps",
    )(
        adjoint_end, jnp.swapaxes(positions, 0, 1), tile_brick, tile_fill.reshape(1, TILES), send_rows,
        source_rows.reshape(TILES, TILE), ckpt_mass, ckpt_velocity,
        ckpt_target.reshape(1, 128), ckpt_brick.reshape(1, 128), gripper_axis.reshape(1, 3),
    )


def solution(mesh):
    return jax.shard_map(
        per_device,
        mesh=mesh,
        in_specs=(
            P(None, ("brick", "slab")),
            P(None, None, ("brick", "slab")),
            P(None, ("brick", "slab")),
            P(("brick", "slab")),
            P(("brick", "slab"), None),
            P(("brick", "slab")),
            P(("brick", "slab"), None),
            P(("brick", "slab"), None),
            P(("brick", "slab")),
            P(("brick", "slab")),
            P(),
        ),
        out_specs=P(None, ("brick", "slab")),
        check_vma=False,
    )
```
